32 devices in a mesh: wa: 4 (over z), facet: 8 (over y, x, core).
Axes of the slice: x: 2, y: 2, z: 4, core: 2. Of those that a mesh axis runs over, the one named last changes fastest.
Arguments:
- visibilities: bfloat16 [4096, 2, 64], P(('wa', 'facet')), may hold values from -6 to 6
- uv_angles: float32 [4096, 2, 64], P(('wa', 'facet')), may hold values from -3.140625 to 3.140625
- routes: int32 [4096, 1], P(('wa', 'facet')), may hold values from 0 to 31; in each aligned block of 128 rows (0 to 127, 128 to 255, ...) at most 8 rows name the same one
- offsets: int32 [4096, 2], P(('wa', 'facet')), may hold values from 0 to 448
- pixel_phase: float32 [8, 512, 512], P('facet'), may hold values from -3.140625 to 3.140625
Outputs:
- partial_images: float32 [4, 8, 512, 1024], P('wa', 'facet')
The draws below stay inside these ranges and needn't reach their ends.
Inputs may be any that keep to these rules, and one draw needn't show every extreme that they name: `routes`: the subgrids of one device name each owner at most 8 times; some owner is named exactly 8 times.
All inputs are finite; a program needn't handle non-finite values.
Results may differ from the reference program's by a relative error of at most 0.0076.
Values may be sent and summed in bfloat16 or wider, within the bound.
No kernel may reach another device: no remote copies, remote signals or barrier semaphores. Data moves between devices by JAX's collectives and lax.ppermute only.
A program may use at most 64 MiB of HBM per device.

```python
import math
import jax
import jax.numpy as jnp
import numpy as np
from jax import lax

SUB = 64
GRID = 512
NVIS = 64
SUB_DEV = 128
OWNERS = 32
FACETS = 8
SUBGRIDS = 4096
CAP = 8
N_WA = 4
N_FACET = 8


def touch_ends(array, key, low, high):
    longest = array.shape.index(max(array.shape))
    spots = []
    for shift in (0, 1):
        where = [jax.random.randint(jax.random.fold_in(key, axis), (), 0, length) for axis, length in enumerate(array.shape)]
        where[longest] = (where[longest] + shift) % array.shape[longest]
        spots.append(tuple(where))
    return array.at[spots[0]].set(low).at[spots[1]].set(high)


def level_of(key, dims, pieces, smallest, top_value):
    gain, own = 1.0, jax.random.fold_in(key, 6)
    for dim, parts in pieces:
        draws = jnp.exp(jax.random.uniform(jax.random.fold_in(own, dim), (parts,), jnp.float32, smallest / len(pieces), top_value / len(pieces)))
        gain = gain * jnp.repeat(draws, dims[dim] // parts).reshape([-1 if axis == dim else 1 for axis in range(len(dims))])
    return gain


def deal_out(own_key, own, number, rows, number_of, top, limit, skew):
    order = jax.random.permutation(own_key, number_of)
    heavy_load, ordinary = load_shares(number_of, rows * top, limit, skew, True), load_shares(number_of, rows * top, limit, skew, False)
    places = jnp.arange(number_of)

    def named(tallies, rotation):
        used = int((tallies > 0).sum())
        fixed = max(1, used // 4)
        passed = fixed + (places - fixed + rotation * (used - fixed)) % max(1, number_of - fixed)
        return jnp.zeros((number_of,), jnp.int32).at[order[jnp.where(places < fixed, places, passed)]].set(jnp.asarray(tallies, jnp.int32))

    tallies = jnp.where(number % 4 == 0, named(heavy_load, number // 4), named(ordinary, number - number // 4 - 1))
    mixed = jax.random.permutation(jax.random.fold_in(own, 3), number_of)
    source_of, sink = mixed[0:number_of // 2 * 2:2], mixed[1:number_of // 2 * 2:2]
    margin = jnp.minimum(tallies[source_of] - 1, limit - tallies[sink]) // 2
    margin = jnp.where((source_of == order[0]) | (sink == order[0]) | (tallies[sink] == 0), 0, jnp.maximum(margin, 0))
    passed = jax.random.randint(jax.random.fold_in(own, 4), (number_of // 2,), 0, 1 << 20) % (margin + 1)
    tallies = tallies.at[source_of].add(-passed).at[sink].add(passed)
    items = jnp.searchsorted(jnp.cumsum(tallies), jnp.arange(rows * top), side="right").astype(jnp.int32)
    listing = items.reshape(top, rows).T
    listing = listing[jax.random.permutation(jax.random.fold_in(own, 1), rows)]
    rotation = jax.random.randint(jax.random.fold_in(own, 2), (rows, 1), 0, top)
    return jnp.take_along_axis(listing, (jnp.arange(top)[None, :] + rotation) % top, axis=1)


def load_shares(count, total, reach, skew, full):
    weights = [(1 << 20) // math.isqrt(rank ** skew) + 1 for rank in range(1, count + 1)]
    largest = reach if full else min(reach, max(-(-total // count), total * weights[0] // sum(weights)))
    least = 1 if total - largest >= count - 1 else 0
    counts, surplus = [largest] + [least] * (count - 1), total - largest - least * (count - 1)
    while surplus > 0:
        free = [i for i in range(1, count) if counts[i] < largest] or [i for i in range(1, count) if counts[i] < reach]
        whole, left = sum([weights[i] for i in free]), surplus
        for i in free:
            extra = min(reach - counts[i], max(1, left * weights[i] // whole), surplus)
            counts[i] = counts[i] + extra
            surplus = surplus - extra
    return np.array(counts)


def normal_values(key, shape, spread, most, split=(), kind=jnp.bfloat16):
    factor_of = level_of(key, shape, split, -0.22, 0.18) if split else 1.0
    drawn = jax.random.normal(key, shape, jnp.float32) * spread * factor_of
    return jnp.minimum(jnp.maximum(drawn, -most), most).astype(kind)


def setup_inputs(seed: int = 0) -> dict:
    streams_of = jax.random.split(jax.random.key(seed), 6)
    visibilities = normal_values(streams_of[0], (SUBGRIDS, 2, NVIS), 1.0, 6.0, ((0, 32),))
    uv_angles = jnp.clip(jax.random.uniform(streams_of[1], (SUBGRIDS, 2, NVIS), jnp.float32, -3.140625, 3.140625), -3.140625, 3.140625)
    routes_keys = jax.random.split(jax.random.fold_in(streams_of[2], 1), SUBGRIDS // SUB_DEV)
    routes_turns = jax.random.permutation(jax.random.fold_in(streams_of[2], 3), SUBGRIDS // SUB_DEV)
    routes = jax.vmap(lambda own, number: deal_out(jax.random.fold_in(streams_of[2], 2), own, number, SUB_DEV, OWNERS, 1, CAP, 2))(routes_keys, routes_turns).reshape((SUBGRIDS, 1))
    offsets = touch_ends(jax.random.randint(streams_of[3], (SUBGRIDS, 2), 0, GRID - SUB + 1), jax.random.fold_in(streams_of[3], 1), 0, GRID - SUB).astype(jnp.int32)
    pixel_phase = jnp.clip(jax.random.uniform(streams_of[4], (FACETS, GRID, GRID), jnp.float32, -3.140625, 3.140625), -3.140625, 3.140625)
    return dict(visibilities=visibilities, uv_angles=uv_angles, routes=routes, offsets=offsets, pixel_phase=pixel_phase)


def form_tables(vis_block, angle_block, sub_n):
    centred = (jnp.arange(sub_n) - sub_n // 2).astype(jnp.float32)
    count_vis = vis_block.shape[2]
    norm_scale = 1.0 / math.sqrt(count_vis)
    phase_u = centred[None, :, None] * angle_block[:, 0][:, None, :]
    phase_v = centred[None, :, None] * angle_block[:, 1][:, None, :]
    cos_u = jnp.cos(phase_u)
    sin_u = jnp.sin(phase_u)
    cos_v = jnp.cos(phase_v)
    sin_v = jnp.sin(phase_v)
    vis_re = vis_block[:, 0].astype(jnp.float32)[:, None, :]
    vis_im = vis_block[:, 1].astype(jnp.float32)[:, None, :]
    left_re = (cos_u * vis_re - sin_u * vis_im) * norm_scale
    left_im = (cos_u * vis_im + sin_u * vis_re) * norm_scale
    left_side = jnp.concatenate([left_re, left_im], axis=2).astype(jnp.bfloat16)
    right_side = jnp.concatenate([jnp.concatenate([cos_v, -sin_v], axis=2), jnp.concatenate([sin_v, cos_v], axis=2)], axis=1).astype(jnp.bfloat16)
    return (left_side, right_side)

def dft_tables(grid_n):
    index_line = jnp.arange(grid_n, dtype=jnp.int32)
    product = index_line[:, None] * index_line[None, :] % grid_n
    angle_table = product.astype(jnp.float32) * (2.0 * math.pi / grid_n)
    root_scale = 1.0 / math.sqrt(grid_n)
    cos_table = jnp.cos(angle_table) * root_scale
    sin_table = jnp.sin(angle_table) * root_scale
    row_table = jnp.concatenate([cos_table, sin_table], axis=0).astype(jnp.bfloat16)
    col_table = jnp.concatenate([jnp.concatenate([cos_table, sin_table], axis=1), jnp.concatenate([-sin_table, cos_table], axis=1)], axis=0).astype(jnp.bfloat16)
    return (row_table, col_table)

def inverse_dft(grid_bf, row_table, col_table, grid_n):
    stacked = jnp.dot(row_table, grid_bf, preferred_element_type=jnp.float32)
    half_re = stacked[:grid_n, :grid_n] - stacked[grid_n:, grid_n:]
    half_im = stacked[:grid_n, grid_n:] + stacked[grid_n:, :grid_n]
    half_band = jnp.concatenate([half_re, half_im], axis=1).astype(jnp.bfloat16)
    return jnp.dot(half_band, col_table, preferred_element_type=jnp.float32)

def phase_times(phase_re, phase_im, field, grid_n):
    field_re = field[..., :grid_n]
    field_im = field[..., grid_n:]
    return jnp.concatenate([phase_re * field_re - phase_im * field_im, phase_re * field_im + phase_im * field_re], axis=-1)

def reference(visibilities, uv_angles, routes, offsets, pixel_phase):
    block_n = 64
    owners_n = N_WA * N_FACET
    count_blocks = SUBGRIDS // block_n
    vis_blocks = visibilities.reshape(count_blocks, block_n, 2, NVIS)
    angle_blocks = uv_angles.reshape(count_blocks, block_n, 2, NVIS)
    route_blocks = routes.reshape(count_blocks, block_n)
    offset_blocks = offsets.reshape(count_blocks, block_n, 2)
    col_base = jnp.arange(2 * SUB, dtype=jnp.int32)
    col_shift = col_base // SUB * GRID + col_base % SUB
    sub_line = jnp.arange(SUB, dtype=jnp.int32)

    def add_block(grids, items):
        vis_block, angle_block, route_block, offset_block = items
        left_side, right_side = form_tables(vis_block, angle_block, SUB)
        subgrids = jnp.einsum('bak,bck->bac', left_side.astype(jnp.float32), right_side.astype(jnp.float32)).astype(jnp.bfloat16)
        owner_index = route_block.astype(jnp.int32)[:, None, None]
        row_index = offset_block[:, 0].astype(jnp.int32)[:, None, None] + sub_line[None, :, None]
        col_index = offset_block[:, 1].astype(jnp.int32)[:, None, None] + col_shift[None, None, :]
        grids = grids.at[owner_index, row_index, col_index].add(subgrids.astype(jnp.float32))
        return (grids, None)
    grids = jnp.zeros((owners_n, GRID, 2 * GRID), jnp.float32)
    grids, _ = lax.scan(add_block, grids, (vis_blocks, angle_blocks, route_blocks, offset_blocks))
    grids_bf = grids.astype(jnp.bfloat16)
    row_table, col_table = dft_tables(GRID)
    images = lax.map(lambda one_grid: inverse_dft(one_grid, row_table, col_table, GRID), grids_bf)
    images = images.reshape(N_WA, N_FACET, GRID, 2 * GRID)
    phase_re = jnp.cos(pixel_phase)
    phase_im = jnp.sin(pixel_phase)
    running = images[0]
    results = [running]
    for plane in range(1, N_WA):
        running = phase_times(phase_re, phase_im, running, GRID) + images[plane]
        results.append(running)
    return jnp.stack(results, axis=0)
```

```python
import functools
import math

import jax
import jax.numpy as jnp
import numpy as np
from jax import lax
from jax.experimental import pallas as pl
from jax.experimental.pallas import tpu as pltpu
from jax.sharding import PartitionSpec as P

SUB = 64
LANES = 128
ROWS = 8
GROUP = 8
CHUNKS = 4
SINE = tuple(
    float(v)
    for v in np.linalg.lstsq(
        *(
            lambda x, w: (
                (x[:, None] ** np.arange(1, 14, 2)[None, :]) * w[:, None],
                np.sin(2 * np.pi * x) * w,
            )
        )(
            0.5 * np.cos(np.pi * (np.arange(2000) + 0.5) / 4000),
            np.ones(2000),
        ),
        rcond=None,
    )[0]
)


def sine_turns(turns):
    x = turns - jnp.round(turns)
    x2 = x * x
    total = jnp.full_like(x, SINE[-1])
    for c in SINE[-2::-1]:
        total = total * x2 + c
    return total * x


def pack_kernel(owners, cap, routes, offsets, angles, vis, out, counts):
    out[...] = jnp.zeros_like(out)

    def clear(i, _):
        counts[i] = 0
        return 0

    lax.fori_loop(0, owners, clear, 0)
    lane = lax.broadcasted_iota(jnp.int32, (1, LANES), 1)

    def place(i, _):
        owner = routes[i]
        rank = counts[owner]
        counts[owner] = rank + 1
        base = owner * (3 * cap) + rank
        out[pl.ds(base, 1), :] = angles[pl.ds(i, 1), :]
        out[pl.ds(base + cap, 1), :] = vis[pl.ds(i, 1), :]
        first, second = offsets[2 * i], offsets[2 * i + 1]
        meta = jnp.where(lane == 0, first, jnp.where(lane == 1, second, 0))
        out[pl.ds(base + 2 * cap, 1), :] = meta.astype(jnp.float32)
        return 0

    lax.fori_loop(0, angles.shape[0], place, 0, unroll=4)


def pack(routes, offsets, angles, vis, owners, cap):
    smem = pl.BlockSpec(memory_space=pltpu.SMEM)
    vmem = pl.BlockSpec(memory_space=pltpu.VMEM)
    return pl.pallas_call(
        functools.partial(pack_kernel, owners, cap),
        out_shape=jax.ShapeDtypeStruct((owners * cap * 3, LANES), jnp.float32),
        in_specs=[smem, smem, vmem, vmem],
        out_specs=vmem,
        scratch_shapes=[pltpu.SMEM((owners,), jnp.int32)],
        name="pack",
    )(routes, offsets, angles, vis)


def image_kernel(
    grid_n, offsets, angles, vis, first_hbm, second_hbm, out,
    tables, turns_u, turns_v, amp_a, amp_b, grid, dense, first, second, sems,
):
    slots = angles.shape[0]
    blocks = grid_n // SUB
    copies = [
        pltpu.make_async_copy(first_hbm, first, sems.at[0]),
        pltpu.make_async_copy(second_hbm, second, sems.at[1]),
    ]
    for copy in copies:
        copy.start()

    lane = lax.broadcasted_iota(jnp.int32, (ROWS, LANES), 1)
    low = lane < SUB
    row = lax.broadcasted_iota(jnp.int32, (ROWS, LANES), 0)
    quarter = jnp.where(low, 0.25, 0.0).astype(jnp.float32)
    sign = jnp.where(low, -1.0, 1.0).astype(jnp.float32)
    row_f = row.astype(jnp.float32)
    steps = row_f * ROWS - SUB // 2

    low_all = lax.broadcasted_iota(jnp.int32, (slots, LANES), 1) < SUB
    both = angles[...] * (1.0 / (2.0 * math.pi))
    swapped = pltpu.roll(both, SUB, 1)
    turns_u[...] = jnp.where(low_all, both, swapped)
    turns_v[...] = jnp.where(low_all, swapped, both)
    both = vis[...] * (1.0 / math.sqrt(SUB))
    swapped = pltpu.roll(both, SUB, 1)
    amp_a[...] = jnp.where(low_all, both, swapped)
    amp_b[...] = jnp.where(low_all, swapped, both)

    def clear(b, _):
        grid[b] = jnp.zeros(grid.shape[1:], grid.dtype)
        return 0

    lax.fori_loop(0, blocks + 1, clear, 0)

    def spread(ref, s):
        return jnp.broadcast_to(ref[pl.ds(s, 1), :], (ROWS, LANES))

    def prepare(s):
        off_u, off_v = offsets[2 * s], offsets[2 * s + 1]
        shift_u = off_u & (ROWS - 1)
        shift_v = off_v & (ROWS - 1)
        step_v = (off_v & (SUB - 1)) // ROWS
        tu, tv = spread(turns_u, s), spread(turns_v, s)
        a, b = spread(amp_a, s), spread(amp_b, s)
        cs = sine_turns(tu * (row - shift_u).astype(jnp.float32) + quarter)
        sc = pltpu.roll(cs, SUB, 1) * sign
        tables[s, 0] = cs * a + sc * b
        tables[s, 1] = sc * a - cs * b
        cs = sine_turns(tu * steps + quarter)
        sc = pltpu.roll(cs, SUB, 1)
        tables[s, 2] = jnp.where(low, cs, sc)
        tables[s, 3] = jnp.where(low, sc, cs)
        cs = sine_turns(tv * ((row - shift_v) & (ROWS - 1)).astype(jnp.float32) + quarter)
        tables[s, 4] = -(cs * sign)
        tables[s, 5] = pltpu.roll(cs, SUB, 1)
        turn = ((row - step_v) & (ROWS - 1)) * ROWS - SUB // 2
        cs = sine_turns(tv * turn.astype(jnp.float32) + quarter)
        sc = pltpu.roll(cs, SUB, 1)
        tables[s, 6] = jnp.where(low, cs, sc)
        tables[s, 7] = jnp.where(low, sc, cs)

    def prepare_group(g, _):
        for i in range(GROUP):
            prepare(g * GROUP + i)
        return 0

    lax.fori_loop(0, slots // GROUP, prepare_group, 0)

    def form(s):
        off_u, off_v = offsets[2 * s], offsets[2 * s + 1]
        shift_u = off_u & (ROWS - 1)
        shift_v = off_v & (ROWS - 1)

        def line(k, j):
            return jnp.broadcast_to(tables[s, k, j : j + 1, :], (ROWS, LANES))

        x, y = tables[s, 0], tables[s, 1]
        pieces = [x * line(2, j) + y * line(3, j) for j in range(SUB // ROWS)]
        last = x * line(2, 0) - y * line(3, 0)
        pieces[0] = jnp.where(row >= shift_u, pieces[0], 0.0)
        pieces.append(jnp.where(row < shift_u, last, 0.0))
        left = jnp.concatenate(pieces, axis=0).astype(jnp.bfloat16)
        x, y = tables[s, 4], tables[s, 5]
        early = row < shift_v
        re, im = [], []
        wr_before, wi_before = line(6, SUB // ROWS - 1), line(7, SUB // ROWS - 1)
        for j in range(SUB // ROWS):
            wr_now, wi_now = line(6, j), line(7, j)
            wr = jnp.where(early, wr_before, wr_now)
            wi = jnp.where(early, wi_before, wi_now)
            re.append(x * wr - y * wi)
            im.append(y * wr + x * wi)
            wr_before, wi_before = wr_now, wi_now
        right = jnp.concatenate(re + im, axis=0).astype(jnp.bfloat16)
        return lax.dot_general(
            left, right, (((1,), (1,)), ((), ())), preferred_element_type=jnp.float32
        )

    lane_cell = lax.broadcasted_iota(jnp.int32, (SUB + ROWS, LANES), 1) & (SUB - 1)

    def add(s, piece):
        off_u, off_v = offsets[2 * s], offsets[2 * s + 1]
        start = pl.multiple_of(off_u // ROWS * ROWS, ROWS)
        block = off_v // SUB
        here = lane_cell >= (off_v & (SUB - 1))
        rows = pl.ds(start, SUB + ROWS)
        grid[block, rows, :] += jnp.where(here, piece, 0.0)
        grid[block + 1, rows, :] += jnp.where(here, 0.0, piece)

    def add_group(g, _):
        formed = [form(g * GROUP + i) for i in range(GROUP)]
        for i in range(GROUP):
            add(g * GROUP + i, formed[i])
        return 0

    lax.fori_loop(0, slots // GROUP, add_group, 0)

    sign_all = jnp.where(lax.broadcasted_iota(jnp.int32, (grid_n, LANES), 1) < SUB, -1.0, 1.0)
    for b in range(blocks):
        cells = grid[b, 0:grid_n, :]
        columns = slice(b * LANES, (b + 1) * LANES)
        dense[0:grid_n, columns] = cells.astype(jnp.bfloat16)
        dense[grid_n : 2 * grid_n, columns] = (pltpu.roll(cells, SUB, 1) * sign_all).astype(
            jnp.bfloat16
        )
    for copy in copies:
        copy.wait()
    step = math.gcd(grid_n, LANES)

    def transform(i, _):
        rows = pl.ds(pl.multiple_of(i * step, step), step)
        half = jnp.dot(first[rows, :], dense[...], preferred_element_type=jnp.float32)
        out[rows, :] = jnp.dot(
            half.astype(jnp.bfloat16), second[...], preferred_element_type=jnp.float32
        )
        return 0

    lax.fori_loop(0, grid_n // step, transform, 0)


def form_image(offsets, angles, vis, first, second, grid_n):
    slots = angles.shape[0]
    blocks = grid_n // SUB
    smem = pl.BlockSpec(memory_space=pltpu.SMEM)
    vmem = pl.BlockSpec(memory_space=pltpu.VMEM)
    anywhere = pl.BlockSpec(memory_space=pl.ANY)
    line = pltpu.VMEM((slots, LANES), jnp.float32)
    return pl.pallas_call(
        functools.partial(image_kernel, grid_n),
        out_shape=jax.ShapeDtypeStruct((grid_n, 2 * grid_n), jnp.float32),
        in_specs=[smem, vmem, vmem, anywhere, anywhere],
        out_specs=vmem,
        scratch_shapes=[
            pltpu.VMEM((slots, 8, ROWS, LANES), jnp.float32),
            line, line, line, line,
            pltpu.VMEM((blocks + 1, grid_n + ROWS, LANES), jnp.float32),
            pltpu.VMEM((2 * grid_n, 2 * grid_n), jnp.bfloat16),
            pltpu.VMEM(first.shape, jnp.bfloat16),
            pltpu.VMEM(second.shape, jnp.bfloat16),
            pltpu.SemaphoreType.DMA((2,)),
        ],
        compiler_params=pltpu.CompilerParams(vmem_limit_bytes=40 * 1024 * 1024),
        name="image",
    )(offsets, angles, vis, first, second)


def dft_tables(grid_n):
    line = np.arange(grid_n)
    angle = (line[:, None] * line[None, :] % grid_n) * (2.0 * np.pi / grid_n)
    cos = np.cos(angle) / math.sqrt(grid_n)
    sin = np.sin(angle) / math.sqrt(grid_n)
    first = np.concatenate([cos, sin], axis=1)
    real = np.concatenate([cos, sin], axis=1).reshape(grid_n // SUB, SUB, 2 * grid_n)
    imag = np.concatenate([-sin, cos], axis=1).reshape(grid_n // SUB, SUB, 2 * grid_n)
    second = np.concatenate([real, imag], axis=1).reshape(2 * grid_n, 2 * grid_n)
    return first.astype(np.float32).astype(jnp.bfloat16), second.astype(np.float32).astype(jnp.bfloat16)


def on_device(visibilities, uv_angles, routes, offsets, pixel_phase):
    sub_count = visibilities.shape[0]
    count_vis = visibilities.shape[2]
    grid_n = pixel_phase.shape[1]
    planes = lax.axis_size("wa")
    owners = planes * lax.axis_size("facet")
    cap = max(2, (2 * sub_count + owners - 1) // owners)
    slots = owners * cap
    sent = pack(
        routes.reshape(sub_count),
        offsets.reshape(2 * sub_count),
        uv_angles.reshape(sub_count, 2 * count_vis),
        visibilities.reshape(sub_count, 2 * count_vis).astype(jnp.float32),
        owners,
        cap,
    )
    got = lax.all_to_all(sent, ("wa", "facet"), split_axis=0, concat_axis=0, tiled=True)
    got = got.reshape(owners, 3, cap, LANES)
    first, second = dft_tables(grid_n)
    image = form_image(
        got[:, 2, :, 0:2].astype(jnp.int32).reshape(2 * slots),
        got[:, 0].reshape(slots, LANES),
        got[:, 1].reshape(slots, LANES),
        jnp.asarray(first),
        jnp.asarray(second),
        grid_n,
    )
    phase_re = jnp.cos(pixel_phase[0])
    phase_im = jnp.sin(pixel_phase[0])
    plane = lax.axis_index("wa")
    rows = grid_n // CHUNKS
    outs = []
    for c in range(CHUNKS):
        part = slice(c * rows, (c + 1) * rows)
        own = image[part]
        running = own
        for hop in range(1, planes):
            incoming = lax.ppermute(
                running.astype(jnp.bfloat16), "wa", [(hop - 1, hop)]
            ).astype(jnp.float32)
            re, im = incoming[:, :grid_n], incoming[:, grid_n:]
            turned = jnp.concatenate(
                [
                    phase_re[part] * re - phase_im[part] * im,
                    phase_re[part] * im + phase_im[part] * re,
                ],
                axis=1,
            )
            running = jnp.where(plane == hop, turned + own, running)
        outs.append(running)
    return jnp.concatenate(outs, axis=0).reshape(1, 1, grid_n, 2 * grid_n)


def solution(mesh):
    in_specs = (
        P(("wa", "facet"), None, None),
        P(("wa", "facet"), None, None),
        P(("wa", "facet"), None),
        P(("wa", "facet"), None),
        P("facet", None, None),
    )
    out_specs = P("wa", "facet", None, None)
    return jax.shard_map(
        on_device, mesh=mesh, in_specs=in_specs, out_specs=out_specs, check_vma=False
    )
```

```python
import functools
import math

import jax
import jax.numpy as jnp
import numpy as np
from jax import lax
from jax.experimental import pallas as pl
from jax.experimental.pallas import tpu as pltpu
from jax.sharding import PartitionSpec as P

SUB = 64
LANES = 128
ROWS = 8
GROUP = 8
PARTS = (7, 7, 7, 6, 5)
SINE = tuple(
    float(v)
    for v in np.linalg.lstsq(
        *(
            lambda x, w: (
                (x[:, None] ** np.arange(1, 14, 2)[None, :]) * w[:, None],
                np.sin(2 * np.pi * x) * w,
            )
        )(
            0.5 * np.cos(np.pi * (np.arange(2000) + 0.5) / 4000),
            np.ones(2000),
        ),
        rcond=None,
    )[0]
)


def sine_turns(turns):
    x = turns - jnp.round(turns)
    x2 = x * x
    total = jnp.full_like(x, SINE[-1])
    for c in SINE[-2::-1]:
        total = total * x2 + c
    return total * x


def pack_kernel(owners, cap, routes, offsets, angles, vis, out, counts, angle_rows, vis_rows):
    out[...] = jnp.zeros_like(out)
    angle_rows[...] = angles[...].T
    vis_rows[...] = vis[...].astype(jnp.float32).T

    def clear(i, _):
        counts[i] = 0
        return 0

    lax.fori_loop(0, owners, clear, 0)
    lane = lax.broadcasted_iota(jnp.int32, (1, LANES), 1)

    def place(i, _):
        owner = routes[0, i]
        rank = counts[owner]
        counts[owner] = rank + 1
        base = owner * (3 * cap) + rank
        out[pl.ds(base, 1), :] = angle_rows[pl.ds(i, 1), :]
        out[pl.ds(base + cap, 1), :] = vis_rows[pl.ds(i, 1), :]
        first, second = offsets[0, i], offsets[1, i]
        meta = jnp.where(lane == 0, first, jnp.where(lane == 1, second, 0))
        out[pl.ds(base + 2 * cap, 1), :] = meta.astype(jnp.float32)
        return 0

    lax.fori_loop(0, angles.shape[1], place, 0, unroll=4)


def pack(routes, offsets, angles, vis, owners, cap):
    smem = pl.BlockSpec(memory_space=pltpu.SMEM)
    vmem = pl.BlockSpec(memory_space=pltpu.VMEM)
    return pl.pallas_call(
        functools.partial(pack_kernel, owners, cap),
        out_shape=jax.ShapeDtypeStruct((owners * cap * 3, LANES), jnp.float32),
        in_specs=[smem, smem, vmem, vmem],
        out_specs=vmem,
        scratch_shapes=[
            pltpu.SMEM((owners,), jnp.int32),
            pltpu.VMEM(angles.shape[::-1], jnp.float32),
            pltpu.VMEM(vis.shape[::-1], jnp.float32),
        ],
        name="pack",
    )(routes, offsets, angles, vis)


def image_kernel(
    grid_n, bounds, offsets, angles, vis, first_hbm, second_hbm, out, *rest
):
    sends = rest[: len(bounds) - 1]
    image_body(grid_n, offsets, angles, vis, first_hbm, second_hbm, out, *rest[len(bounds) - 1 :])
    for i, send in enumerate(sends):
        send[...] = out[bounds[i] : bounds[i + 1], :].astype(jnp.bfloat16)


def image_body(
    grid_n, offsets, angles, vis, first_hbm, second_hbm, out,
    tables, turns_u, turns_v, amp_a, amp_b, grid, dense, first, second, sems,
):
    slots = angles.shape[0]
    blocks = grid_n // SUB
    copies = [
        pltpu.make_async_copy(first_hbm, first, sems.at[0]),
        pltpu.make_async_copy(second_hbm, second, sems.at[1]),
    ]
    for copy in copies:
        copy.start()

    lane = lax.broadcasted_iota(jnp.int32, (ROWS, LANES), 1)
    low = lane < SUB
    row = lax.broadcasted_iota(jnp.int32, (ROWS, LANES), 0)
    quarter = jnp.where(low, 0.25, 0.0).astype(jnp.float32)
    sign = jnp.where(low, -1.0, 1.0).astype(jnp.float32)
    row_f = row.astype(jnp.float32)
    steps = row_f * ROWS - SUB // 2

    low_all = lax.broadcasted_iota(jnp.int32, (slots, LANES), 1) < SUB
    both = angles[...] * (1.0 / (2.0 * math.pi))
    swapped = pltpu.roll(both, SUB, 1)
    turns_u[...] = jnp.where(low_all, both, swapped)
    turns_v[...] = jnp.where(low_all, swapped, both)
    both = vis[...] * (1.0 / math.sqrt(SUB))
    swapped = pltpu.roll(both, SUB, 1)
    amp_a[...] = jnp.where(low_all, both, swapped)
    amp_b[...] = jnp.where(low_all, swapped, both)

    def clear(b, _):
        grid[b] = jnp.zeros(grid.shape[1:], grid.dtype)
        return 0

    lax.fori_loop(0, blocks + 1, clear, 0)

    def spread(ref, s):
        return jnp.broadcast_to(ref[pl.ds(s, 1), :], (ROWS, LANES))

    def prepare(s):
        off_u, off_v = offsets[2 * s], offsets[2 * s + 1]
        shift_u = off_u & (ROWS - 1)
        shift_v = off_v & (ROWS - 1)
        step_v = (off_v & (SUB - 1)) // ROWS
        tu, tv = spread(turns_u, s), spread(turns_v, s)
        a, b = spread(amp_a, s), spread(amp_b, s)
        cs = sine_turns(tu * (row - shift_u).astype(jnp.float32) + quarter)
        sc = pltpu.roll(cs, SUB, 1) * sign
        tables[s, 0] = cs * a + sc * b
        tables[s, 1] = sc * a - cs * b
        cs = sine_turns(tu * steps + quarter)
        sc = pltpu.roll(cs, SUB, 1)
        tables[s, 2] = jnp.where(low, cs, sc)
        tables[s, 3] = jnp.where(low, sc, cs)
        cs = sine_turns(tv * ((row - shift_v) & (ROWS - 1)).astype(jnp.float32) + quarter)
        tables[s, 4] = -(cs * sign)
        tables[s, 5] = pltpu.roll(cs, SUB, 1)
        turn = ((row - step_v) & (ROWS - 1)) * ROWS - SUB // 2
        cs = sine_turns(tv * turn.astype(jnp.float32) + quarter)
        sc = pltpu.roll(cs, SUB, 1)
        tables[s, 6] = jnp.where(low, cs, sc)
        tables[s, 7] = jnp.where(low, sc, cs)

    def prepare_group(g, _):
        for i in range(GROUP):
            prepare(g * GROUP + i)
        return 0

    lax.fori_loop(0, slots // GROUP, prepare_group, 0)

    def form(s):
        off_u, off_v = offsets[2 * s], offsets[2 * s + 1]
        shift_u = off_u & (ROWS - 1)
        shift_v = off_v & (ROWS - 1)

        def line(k, j):
            return jnp.broadcast_to(tables[s, k, j : j + 1, :], (ROWS, LANES))

        x, y = tables[s, 0], tables[s, 1]
        pieces = [x * line(2, j) + y * line(3, j) for j in range(SUB // ROWS)]
        last = x * line(2, 0) - y * line(3, 0)
        pieces[0] = jnp.where(row >= shift_u, pieces[0], 0.0)
        pieces.append(jnp.where(row < shift_u, last, 0.0))
        left = jnp.concatenate(pieces, axis=0).astype(jnp.bfloat16)
        x, y = tables[s, 4], tables[s, 5]
        early = row < shift_v
        re, im = [], []
        wr_before, wi_before = line(6, SUB // ROWS - 1), line(7, SUB // ROWS - 1)
        for j in range(SUB // ROWS):
            wr_now, wi_now = line(6, j), line(7, j)
            wr = jnp.where(early, wr_before, wr_now)
            wi = jnp.where(early, wi_before, wi_now)
            re.append(x * wr - y * wi)
            im.append(y * wr + x * wi)
            wr_before, wi_before = wr_now, wi_now
        right = jnp.concatenate(re + im, axis=0).astype(jnp.bfloat16)
        return lax.dot_general(
            left, right, (((1,), (1,)), ((), ())), preferred_element_type=jnp.float32
        )

    lane_cell = lax.broadcasted_iota(jnp.int32, (SUB + ROWS, LANES), 1) & (SUB - 1)

    def add(s, piece):
        off_u, off_v = offsets[2 * s], offsets[2 * s + 1]
        start = pl.multiple_of(off_u // ROWS * ROWS, ROWS)
        block = off_v // SUB
        here = lane_cell >= (off_v & (SUB - 1))
        rows = pl.ds(start, SUB + ROWS)
        grid[block, rows, :] += jnp.where(here, piece, 0.0)
        grid[block + 1, rows, :] += jnp.where(here, 0.0, piece)

    def add_group(g, _):
        formed = [form(g * GROUP + i) for i in range(GROUP)]
        for i in range(GROUP):
            add(g * GROUP + i, formed[i])
        return 0

    lax.fori_loop(0, slots // GROUP, add_group, 0)

    sign_all = jnp.where(lax.broadcasted_iota(jnp.int32, (grid_n, LANES), 1) < SUB, -1.0, 1.0)
    for b in range(blocks):
        cells = grid[b, 0:grid_n, :]
        columns = slice(b * LANES, (b + 1) * LANES)
        dense[0:grid_n, columns] = cells.astype(jnp.bfloat16)
        dense[grid_n : 2 * grid_n, columns] = (pltpu.roll(cells, SUB, 1) * sign_all).astype(
            jnp.bfloat16
        )
    for copy in copies:
        copy.wait()
    step = math.gcd(grid_n, LANES)

    def transform(i, _):
        rows = pl.ds(pl.multiple_of(i * step, step), step)
        half = jnp.dot(first[rows, :], dense[...], preferred_element_type=jnp.float32)
        out[rows, :] = jnp.dot(
            half.astype(jnp.bfloat16), second[...], preferred_element_type=jnp.float32
        )
        return 0

    lax.fori_loop(0, grid_n // step, transform, 0)


def form_image(offsets, angles, vis, first, second, grid_n, bounds):
    slots = angles.shape[0]
    blocks = grid_n // SUB
    smem = pl.BlockSpec(memory_space=pltpu.SMEM)
    vmem = pl.BlockSpec(memory_space=pltpu.VMEM)
    hbm = pl.BlockSpec(memory_space=pltpu.HBM)
    line = pltpu.VMEM((slots, LANES), jnp.float32)
    return pl.pallas_call(
        functools.partial(image_kernel, grid_n, bounds),
        out_shape=[pltpu.VMEM((grid_n, 2 * grid_n), jnp.float32)]
        + [pltpu.VMEM((b - a, 2 * grid_n), jnp.bfloat16) for a, b in zip(bounds, bounds[1:])],
        in_specs=[smem, vmem, vmem, hbm, hbm],
        out_specs=[vmem] * len(bounds),
        scratch_shapes=[
            pltpu.VMEM((slots, 8, ROWS, LANES), jnp.float32),
            line, line, line, line,
            pltpu.VMEM((blocks + 1, grid_n + ROWS, LANES), jnp.float32),
            pltpu.VMEM((2 * grid_n, 2 * grid_n), jnp.bfloat16),
            pltpu.VMEM(first.shape, jnp.bfloat16),
            pltpu.VMEM(second.shape, jnp.bfloat16),
            pltpu.SemaphoreType.DMA((2,)),
        ],
        compiler_params=pltpu.CompilerParams(vmem_limit_bytes=32 * 1024 * 1024),
        name="image",
    )(offsets, angles, vis, first, second)


def dft_tables(grid_n):
    line = np.arange(grid_n)
    angle = (line[:, None] * line[None, :] % grid_n) * (2.0 * np.pi / grid_n)
    cos = np.cos(angle) / math.sqrt(grid_n)
    sin = np.sin(angle) / math.sqrt(grid_n)
    first = np.concatenate([cos, sin], axis=1)
    real = np.concatenate([cos, sin], axis=1).reshape(grid_n // SUB, SUB, 2 * grid_n)
    imag = np.concatenate([-sin, cos], axis=1).reshape(grid_n // SUB, SUB, 2 * grid_n)
    second = np.concatenate([real, imag], axis=1).reshape(2 * grid_n, 2 * grid_n)
    return first.astype(np.float32).astype(jnp.bfloat16), second.astype(np.float32).astype(jnp.bfloat16)


def phase_kernel(phase, turns):
    grid_n = phase.shape[1]
    step = math.gcd(grid_n, LANES)

    def some(i, _):
        rows = pl.ds(pl.multiple_of(i * step, step), step)
        part = phase[rows, :] * (1.0 / (2.0 * math.pi))
        turns[rows, :grid_n] = sine_turns(part + 0.25)
        turns[rows, grid_n:] = sine_turns(part)
        return 0

    lax.fori_loop(0, grid_n // step, some, 0)


def phase_tables(phase):
    grid_n = phase.shape[1]
    vmem = pl.BlockSpec(memory_space=pltpu.VMEM)
    return pl.pallas_call(
        phase_kernel,
        out_shape=pltpu.VMEM((grid_n, 2 * grid_n), jnp.float32),
        in_specs=[vmem],
        out_specs=vmem,
        compiler_params=pltpu.CompilerParams(vmem_limit_bytes=8 * 1024 * 1024),
        name="phases",
    )(phase)


def send_up(part, hop):
    return lax.ppermute(part, "wa", [(hop - 1, hop)])


def horner_kernel(hop, start, incoming, image, turns, *outs):
    grid_n = image.shape[1] // 2
    rows = pl.ds(start, incoming.shape[0])
    re_cells, im_cells = pl.ds(0, grid_n), pl.ds(grid_n, grid_n)

    @pl.when(lax.axis_index("wa") == hop)
    def _():
        re = incoming[:, re_cells].astype(jnp.float32)
        im = incoming[:, im_cells].astype(jnp.float32)
        turn_re, turn_im = turns[rows, re_cells], turns[rows, im_cells]
        new_re = turn_re * re - turn_im * im + image[rows, re_cells]
        new_im = turn_re * im + turn_im * re + image[rows, im_cells]
        outs[-1][rows, re_cells] = new_re
        outs[-1][rows, im_cells] = new_im
        for send in outs[:-1]:
            send[:, re_cells] = new_re.astype(jnp.bfloat16)
            send[:, im_cells] = new_im.astype(jnp.bfloat16)


def horner_step(hop, planes, start, end, incoming, image, turns):
    vmem = pl.BlockSpec(memory_space=pltpu.VMEM)
    outs = [pltpu.VMEM((end - start, image.shape[1]), jnp.bfloat16)] * (hop + 1 < planes)
    outs.append(pltpu.VMEM(image.shape, jnp.float32))
    got = pl.pallas_call(
        functools.partial(horner_kernel, hop, start),
        out_shape=outs,
        in_specs=[vmem] * 3,
        out_specs=[vmem] * len(outs),
        input_output_aliases={1: len(outs) - 1},
        compiler_params=pltpu.CompilerParams(vmem_limit_bytes=4 * 1024 * 1024),
        name="horner",
    )(*(pltpu.with_memory_space_constraint(x, pltpu.VMEM) for x in (incoming, image, turns)))
    return got[0], got[-1]


def on_device(visibilities, uv_angles, routes, offsets, pixel_phase):
    sub_count = visibilities.shape[0]
    count_vis = visibilities.shape[2]
    grid_n = pixel_phase.shape[1]
    planes = lax.axis_size("wa")
    owners = planes * lax.axis_size("facet")
    cap = max(2, (2 * sub_count + owners - 1) // owners)
    slots = owners * cap
    sent = pack(
        routes.T,
        offsets.T,
        uv_angles.transpose(1, 2, 0).reshape(2 * count_vis, sub_count),
        visibilities.transpose(1, 2, 0).reshape(2 * count_vis, sub_count),
        owners,
        cap,
    )
    got = lax.all_to_all(sent, ("wa", "facet"), split_axis=0, concat_axis=0, tiled=True)
    got = got.reshape(owners, 3, cap, LANES)
    first, second = dft_tables(grid_n)
    units = grid_n // 16
    bounds = [0] + [16 * (units * sum(PARTS[: i + 1]) // sum(PARTS)) for i in range(len(PARTS))]
    image, *sends = form_image(
        got[:, 2, :, 0:2].astype(jnp.int32).reshape(2 * slots),
        got[:, 0].reshape(slots, LANES),
        got[:, 1].reshape(slots, LANES),
        jnp.asarray(first),
        jnp.asarray(second),
        grid_n,
        bounds,
    )
    turns = phase_tables(pixel_phase[0])
    incoming = {(1, c): send_up(sends[c], 1) for c in range(len(sends))}
    for beat in range(len(sends) + 2 * planes):
        for hop in range(1, planes):
            c = beat - 2 * (hop - 1)
            if 0 <= c < len(sends):
                send, image = horner_step(
                    hop, planes, bounds[c], bounds[c + 1], incoming[hop, c], image, turns
                )
                if hop + 1 < planes:
                    incoming[hop + 1, c] = send_up(send, hop + 1)
    return image.reshape(1, 1, grid_n, 2 * grid_n)


def solution(mesh):
    in_specs = (
        P(("wa", "facet"), None, None),
        P(("wa", "facet"), None, None),
        P(("wa", "facet"), None),
        P(("wa", "facet"), None),
        P("facet", None, None),
    )
    out_specs = P("wa", "facet", None, None)
    return jax.shard_map(
        on_device, mesh=mesh, in_specs=in_specs, out_specs=out_specs, check_vma=False
    )
```

```python
import functools
import math

import jax
import jax.numpy as jnp
import numpy as np
from jax import lax
from jax.experimental import pallas as pl
from jax.experimental.pallas import tpu as pltpu
from jax.sharding import PartitionSpec as P

SUB = 64
LANES = 128
ROWS = 8
GROUP = 8
PARTS = (7, 7, 7, 6, 5)
AHEAD = 2
LAG = 2
DIGITS = 3
DIGIT = 16.0
SINE = tuple(
    float(v)
    for v in np.linalg.lstsq(
        *(
            lambda x, w: (
                (x[:, None] ** np.arange(1, 10, 2)[None, :]) * w[:, None],
                np.sin(2 * np.pi * x) * w,
            )
        )(
            0.5 * np.cos(np.pi * (np.arange(2000) + 0.5) / 4000),
            np.ones(2000),
        ),
        rcond=None,
    )[0]
)


def sine_turns(turns):
    x = turns - jnp.round(turns)
    x2 = x * x
    total = jnp.full_like(x, SINE[-1])
    for c in SINE[-2::-1]:
        total = total * x2 + c
    return total * x


def pack_kernel(owners, cap, routes, offsets, angles, vis, out, counts, angle_rows, vis_rows):
    out[...] = jnp.zeros_like(out)
    angle_rows[...] = angles[...].T
    values = vis[...].astype(jnp.float32)
    spot = lax.broadcasted_iota(jnp.int32, values.shape, 0)
    for axis in range(2):
        for place in range(DIGITS):
            digit = (offsets[axis : axis + 1, :] >> (3 * place)) & 7
            carried = jnp.where(spot == axis * DIGITS + place, digit, 0)
            values = values + carried.astype(jnp.float32) * DIGIT
    vis_rows[...] = values.T

    def clear(i, _):
        counts[i] = 0
        return 0

    lax.fori_loop(0, owners, clear, 0)

    def place_row(i, _):
        owner = routes[0, i]
        rank = counts[owner]
        counts[owner] = rank + 1
        base = owner * (2 * cap) + rank
        out[pl.ds(base, 1), :] = angle_rows[pl.ds(i, 1), :]
        out[pl.ds(base + cap, 1), :] = vis_rows[pl.ds(i, 1), :]
        return 0

    lax.fori_loop(0, angles.shape[1], place_row, 0, unroll=8)


def pack(routes, offsets, angles, vis, owners, cap):
    smem = pl.BlockSpec(memory_space=pltpu.SMEM)
    vmem = pl.BlockSpec(memory_space=pltpu.VMEM)
    return pl.pallas_call(
        functools.partial(pack_kernel, owners, cap),
        out_shape=jax.ShapeDtypeStruct((owners * cap * 2, LANES), jnp.float32),
        in_specs=[smem, vmem, vmem, vmem],
        out_specs=vmem,
        scratch_shapes=[
            pltpu.SMEM((owners,), jnp.int32),
            pltpu.VMEM(angles.shape[::-1], jnp.float32),
            pltpu.VMEM(vis.shape[::-1], jnp.float32),
        ],
        name="pack",
    )(routes, offsets, angles, vis)


def grid_kernel(
    owners, offsets, got, first_hbm, second_hbm, dense, first, second,
    turns_u, turns_v, amp_a, amp_b, grid, sems, *stages,
):
    slots = got.shape[0] // 2
    cap = slots // owners
    grid_n = dense.shape[0]
    blocks = grid_n // SUB
    group = stages[0].shape[0]
    groups = slots // group
    bases, lefts, rights, pieces = (stages[2 * k : 2 * k + 2] for k in range(4))
    copies = [
        pltpu.make_async_copy(first_hbm, first, sems.at[0]),
        pltpu.make_async_copy(second_hbm, second, sems.at[1]),
    ]
    for copy in copies:
        copy.start()

    lane = lax.broadcasted_iota(jnp.int32, (ROWS, LANES), 1)
    low = lane < SUB
    row = lax.broadcasted_iota(jnp.int32, (ROWS, LANES), 0)
    quarter = jnp.where(low, 0.25, 0.0).astype(jnp.float32)
    sign = jnp.where(low, -1.0, 1.0).astype(jnp.float32)
    row_f = row.astype(jnp.float32)
    upper = row < ROWS // 2
    eights = ((row & (ROWS // 2 - 1)) * ROWS + ROWS).astype(jnp.float32)
    middle = SUB // ROWS // 2

    low_cap = lax.broadcasted_iota(jnp.int32, (cap, LANES), 1) < SUB

    def spread_out(i, _):
        angles = got[pl.ds(i * (2 * cap), cap), :]
        vis = got[pl.ds(i * (2 * cap) + cap, cap), :]
        vis = vis - jnp.round(vis * (1.0 / DIGIT)) * DIGIT
        rows = pl.ds(i * cap, cap)
        both = angles * (1.0 / (2.0 * math.pi))
        swapped = pltpu.roll(both, SUB, 1)
        turns_u[rows, :] = jnp.where(low_cap, both, swapped)
        turns_v[rows, :] = jnp.where(low_cap, swapped, both)
        both = vis * (1.0 / math.sqrt(SUB))
        swapped = pltpu.roll(both, SUB, 1)
        amp_a[rows, :] = jnp.where(low_cap, both, swapped)
        amp_b[rows, :] = jnp.where(low_cap, swapped, both)
        return 0

    lax.fori_loop(0, owners, spread_out, 0, unroll=8)

    def clear(b, _):
        grid[b] = jnp.zeros(grid.shape[1:], grid.dtype)
        return 0

    lax.fori_loop(0, blocks + 1, clear, 0)

    def spread(ref, s):
        return jnp.broadcast_to(ref[pl.ds(s, 1), :], (ROWS, LANES))

    def find_bases(g, out):
        for i in range(group):
            s = g * group + i
            tu, tv = spread(turns_u, s), spread(turns_v, s)
            a, b = spread(amp_a, s), spread(amp_b, s)
            cs = sine_turns(tu * row_f + quarter)
            sc = pltpu.roll(cs, SUB, 1) * sign
            out[i, 0] = cs * a + sc * b
            out[i, 1] = sc * a - cs * b
            cs = sine_turns(tv * row_f + quarter)
            out[i, 2] = -(cs * sign)
            out[i, 3] = pltpu.roll(cs, SUB, 1)
            cs = sine_turns(jnp.where(upper, tu, tv) * eights + quarter)
            sc = pltpu.roll(cs, SUB, 1)
            out[i, 4] = jnp.where(low, cs, sc)
            out[i, 5] = jnp.where(low, sc, cs)

    def find_rows(source, left, right):
        for i in range(group):

            def line(k, j):
                return jnp.broadcast_to(source[i, k, j : j + 1, :], (ROWS, LANES))

            x, y = source[i, 0], source[i, 1]
            parts = [x]
            for j in range(middle):
                along, across = x * line(4, j), y * line(5, j)
                parts = [along - across] + parts
                if j + 1 < middle:
                    parts = parts + [along + across]
            left[i] = jnp.concatenate(parts, axis=0).astype(jnp.bfloat16)

            def keep(k, value_re, value_im):
                places = (0, 2 * middle) if k == 0 else (k,)
                for place in places:
                    right[i, 0, place * ROWS : (place + 1) * ROWS, :] = value_re
                    right[i, 1, place * ROWS : (place + 1) * ROWS, :] = value_im

            x, y = source[i, 2], source[i, 3]
            keep(middle, x, y)
            for j in range(middle):
                wr, wi = line(4, middle + j), line(5, middle + j)
                xr, xi, yr, yi = x * wr, x * wi, y * wr, y * wi
                keep(middle - 1 - j, xr + yi, yr - xi)
                if j + 1 < middle:
                    keep(middle + 1 + j, xr - yi, yr + xi)

    def multiply(g, left, right, out):
        for i in range(group):
            shift = offsets[2 * (g * group + i) + 1] & (SUB - 1)
            parts = [
                right[i, k, pl.ds((j * ROWS - shift) & (SUB - 1), ROWS), :]
                for k in range(2)
                for j in range(SUB // ROWS)
            ]
            turned = jnp.concatenate(parts, axis=0).astype(jnp.bfloat16)
            out[i] = lax.dot_general(
                left[i], turned, (((1,), (1,)), ((), ())), preferred_element_type=jnp.float32
            )

    cell = lane & (SUB - 1)

    def add(g, formed):
        for i in range(group):
            s = g * group + i
            off_u, off_v = offsets[2 * s], offsets[2 * s + 1]
            block = off_v // SUB
            here = cell >= (off_v & (SUB - 1))
            for side in range(2):
                for j in range(SUB // ROWS):
                    place = grid.at[block + side, pl.ds(off_u + j * ROWS, ROWS), :]
                    total = place[...] + formed[i, j * ROWS : (j + 1) * ROWS, :]
                    pltpu.store(place, total, mask=~here if side else here)

    pieces[0][...] = jnp.zeros_like(pieces[0])
    lefts[1][...] = jnp.zeros_like(lefts[1])
    rights[1][...] = jnp.zeros_like(rights[1])
    find_bases(0, bases[0])

    def pair(p, _):
        for k in range(2):
            g = 2 * p + k
            add(jnp.maximum(g - 2, 0), pieces[k])
            multiply(jnp.maximum(g - 1, 0), lefts[1 - k], rights[1 - k], pieces[1 - k])
            find_rows(bases[k], lefts[k], rights[k])
            find_bases(jnp.minimum(g + 1, groups - 1), bases[1 - k])
        return 0

    lax.fori_loop(0, groups // 2, pair, 0)
    add(groups - 2, pieces[0])
    multiply(groups - 1, lefts[1], rights[1], pieces[1])
    add(groups - 1, pieces[1])

    for b in range(blocks):
        dense[:, b * LANES : (b + 1) * LANES] = grid[b].astype(jnp.bfloat16)
    for copy in copies:
        copy.wait()


def form_grid(offsets, got, first, second, owners):
    slots = got.shape[0] // 2
    grid_n = first.shape[0]
    blocks = grid_n // SUB
    group = math.gcd(slots // 2, GROUP)
    smem = pl.BlockSpec(memory_space=pltpu.SMEM)
    vmem = pl.BlockSpec(memory_space=pltpu.VMEM)
    hbm = pl.BlockSpec(memory_space=pltpu.HBM)
    line = pltpu.VMEM((slots, LANES), jnp.float32)
    stages = [
        pltpu.VMEM((group, 6, ROWS, LANES), jnp.float32),
        pltpu.VMEM((group, SUB, LANES), jnp.bfloat16),
        pltpu.VMEM((group, 2, SUB + ROWS, LANES), jnp.float32),
        pltpu.VMEM((group, SUB, LANES), jnp.float32),
    ]
    return pl.pallas_call(
        functools.partial(grid_kernel, owners),
        out_shape=[
            pltpu.VMEM((grid_n, 2 * grid_n), jnp.bfloat16),
            pltpu.VMEM(first.shape, jnp.bfloat16),
            pltpu.VMEM(second.shape, jnp.bfloat16),
        ],
        in_specs=[smem, vmem, hbm, hbm],
        out_specs=[vmem] * 3,
        scratch_shapes=[
            line, line, line, line,
            pltpu.VMEM((blocks + 1, grid_n, LANES), jnp.float32),
            pltpu.SemaphoreType.DMA((2,)),
            *(stage for stage in stages for _ in range(2)),
        ],
        compiler_params=pltpu.CompilerParams(vmem_limit_bytes=24 * 1024 * 1024),
        name="grid",
    )(
        offsets,
        got,
        pltpu.with_memory_space_constraint(first, pltpu.HBM),
        pltpu.with_memory_space_constraint(second, pltpu.HBM),
    )


def transform_rows(dense, first, second, start, end):
    grid_n = dense.shape[0]
    rows = end - start
    both = jnp.concatenate([first[start:end, :grid_n], first[start:end, grid_n:]], axis=0)
    both = jnp.dot(both, dense[...], preferred_element_type=jnp.float32)
    sign = jnp.where(lax.broadcasted_iota(jnp.int32, (rows, LANES), 1) < SUB, -1.0, 1.0)
    half = [
        both[:rows, at : at + LANES] + pltpu.roll(both[rows:, at : at + LANES], SUB, 1) * sign
        for at in range(0, 2 * grid_n, LANES)
    ]
    half = jnp.concatenate(half, axis=1).astype(jnp.bfloat16)
    return jnp.dot(half, second[...], preferred_element_type=jnp.float32)


def first_rows_kernel(end, dense, first, second, image, send):
    rows = transform_rows(dense, first, second, 0, end)
    image[0:end, :] = rows
    send[...] = rows.astype(jnp.bfloat16)


def turn_rows(phase, turns, start, end):
    grid_n = phase.shape[1]
    part = phase[start:end, :] * (1.0 / (2.0 * math.pi))
    turns[start:end, :grid_n] = sine_turns(part + 0.25)
    turns[start:end, grid_n:] = sine_turns(part)


def other_rows_kernel(bounds, phase, dense, first, second, _, image, turns):
    turn_rows(phase, turns, 0, bounds[1])
    for start, end in zip(bounds[1:], bounds[2:]):
        image[start:end, :] = transform_rows(dense, first, second, start, end)
        turn_rows(phase, turns, start, end)


def pinned(*arrays):
    return [pltpu.with_memory_space_constraint(x, pltpu.VMEM) for x in arrays]


def first_rows(dense, first, second, end):
    grid_n = first.shape[0]
    vmem = pl.BlockSpec(memory_space=pltpu.VMEM)
    return pl.pallas_call(
        functools.partial(first_rows_kernel, end),
        out_shape=[
            pltpu.VMEM((grid_n, 2 * grid_n), jnp.float32),
            pltpu.VMEM((end, 2 * grid_n), jnp.bfloat16),
        ],
        in_specs=[vmem] * 3,
        out_specs=[vmem] * 2,
        compiler_params=pltpu.CompilerParams(vmem_limit_bytes=8 * 1024 * 1024),
        name="first_rows",
    )(*pinned(dense, first, second))


def other_rows(phase, dense, first, second, image, bounds):
    vmem = pl.BlockSpec(memory_space=pltpu.VMEM)
    return pl.pallas_call(
        functools.partial(other_rows_kernel, bounds),
        out_shape=[pltpu.VMEM(image.shape, jnp.float32), pltpu.VMEM(image.shape, jnp.float32)],
        in_specs=[vmem] * 5,
        out_specs=[vmem] * 2,
        input_output_aliases={4: 0},
        compiler_params=pltpu.CompilerParams(vmem_limit_bytes=8 * 1024 * 1024),
        name="other_rows",
    )(*pinned(phase, dense, first, second, image))


def dft_tables(grid_n):
    line = np.arange(grid_n)
    angle = (line[:, None] * line[None, :] % grid_n) * (2.0 * np.pi / grid_n)
    cos = np.cos(angle) / math.sqrt(grid_n)
    sin = np.sin(angle) / math.sqrt(grid_n)
    first = np.concatenate([cos, sin], axis=1)
    real = np.concatenate([cos, sin], axis=1).reshape(grid_n // SUB, SUB, 2 * grid_n)
    imag = np.concatenate([-sin, cos], axis=1).reshape(grid_n // SUB, SUB, 2 * grid_n)
    second = np.concatenate([real, imag], axis=1).reshape(2 * grid_n, 2 * grid_n)
    return first.astype(np.float32).astype(jnp.bfloat16), second.astype(np.float32).astype(jnp.bfloat16)


def send_up(part, hop):
    return lax.ppermute(part, "wa", [(hop - 1, hop)])


def horner_kernel(hop, start, incoming, image, turns, *outs):
    grid_n = image.shape[1] // 2
    rows = pl.ds(start, incoming.shape[0])
    re_cells, im_cells = pl.ds(0, grid_n), pl.ds(grid_n, grid_n)

    @pl.when(lax.axis_index("wa") == hop)
    def _():
        re = incoming[:, re_cells].astype(jnp.float32)
        im = incoming[:, im_cells].astype(jnp.float32)
        turn_re, turn_im = turns[rows, re_cells], turns[rows, im_cells]
        new_re = turn_re * re - turn_im * im + image[rows, re_cells]
        new_im = turn_re * im + turn_im * re + image[rows, im_cells]
        outs[-1][rows, re_cells] = new_re
        outs[-1][rows, im_cells] = new_im
        for send in outs[:-1]:
            send[:, re_cells] = new_re.astype(jnp.bfloat16)
            send[:, im_cells] = new_im.astype(jnp.bfloat16)


def horner_step(hop, planes, start, end, incoming, image, turns):
    vmem = pl.BlockSpec(memory_space=pltpu.VMEM)
    outs = [pltpu.VMEM((end - start, image.shape[1]), jnp.bfloat16)] * (hop + 1 < planes)
    outs.append(pltpu.VMEM(image.shape, jnp.float32))
    got = pl.pallas_call(
        functools.partial(horner_kernel, hop, start),
        out_shape=outs,
        in_specs=[vmem] * 3,
        out_specs=[vmem] * len(outs),
        input_output_aliases={1: len(outs) - 1},
        compiler_params=pltpu.CompilerParams(vmem_limit_bytes=4 * 1024 * 1024),
        name="horner",
    )(*pinned(incoming, image, turns))
    return got[0], got[-1]


def begin_kernel(start, image, send, _):
    @pl.when(lax.axis_index("wa") == 0)
    def _():
        send[...] = image[pl.ds(start, send.shape[0]), :].astype(jnp.bfloat16)


def begin_chain(start, end, image):
    vmem = pl.BlockSpec(memory_space=pltpu.VMEM)
    return pl.pallas_call(
        functools.partial(begin_kernel, start),
        out_shape=[
            pltpu.VMEM((end - start, image.shape[1]), jnp.bfloat16),
            pltpu.VMEM(image.shape, jnp.float32),
        ],
        in_specs=[vmem],
        out_specs=[vmem] * 2,
        input_output_aliases={0: 1},
        compiler_params=pltpu.CompilerParams(vmem_limit_bytes=4 * 1024 * 1024),
        name="begin",
    )(*pinned(image))


def on_device(visibilities, uv_angles, routes, offsets, pixel_phase):
    sub_count = visibilities.shape[0]
    count_vis = visibilities.shape[2]
    grid_n = pixel_phase.shape[1]
    planes = lax.axis_size("wa")
    owners = planes * lax.axis_size("facet")
    cap = max(2, (2 * sub_count + owners - 1) // owners)
    slots = owners * cap
    sent = pack(
        routes.T,
        offsets.T,
        uv_angles.transpose(1, 2, 0).reshape(2 * count_vis, sub_count),
        visibilities.transpose(1, 2, 0).reshape(2 * count_vis, sub_count),
        owners,
        cap,
    )
    got = lax.all_to_all(sent, ("wa", "facet"), split_axis=0, concat_axis=0, tiled=True)
    digits = got.reshape(owners, 2, cap, LANES)[:, 1, :, : 2 * DIGITS]
    digits = jnp.round(digits * (1.0 / DIGIT)).astype(jnp.int32).reshape(slots, 2, DIGITS)
    own_offsets = digits[:, :, 0]
    for place in range(1, DIGITS):
        own_offsets = own_offsets + (digits[:, :, place] << (3 * place))
    first, second = (jnp.asarray(x) for x in dft_tables(grid_n))
    dense, first, second = form_grid(own_offsets.reshape(2 * slots), got, first, second, owners)

    units = grid_n // 16
    bounds = [0] + [16 * (units * sum(PARTS[: i + 1]) // sum(PARTS)) for i in range(len(PARTS))]
    count = len(PARTS)
    image, send = first_rows(dense, first, second, bounds[1])
    incoming = {(1, 0): send_up(send, 1)}
    image, turns = other_rows(pixel_phase[0], dense, first, second, image, bounds)

    def begin(c, image):
        if c < count:
            send, image = begin_chain(bounds[c], bounds[c + 1], image)
            incoming[1, c] = send_up(send, 1)
        return image

    for c in range(1, AHEAD):
        image = begin(c, image)
    for beat in range(count + LAG * planes):
        for hop in range(1, planes):
            c = beat - LAG * (hop - 1)
            if 0 <= c < count:
                send, image = horner_step(
                    hop, planes, bounds[c], bounds[c + 1], incoming[hop, c], image, turns
                )
                if hop + 1 < planes:
                    incoming[hop + 1, c] = send_up(send, hop + 1)
                if hop == 1:
                    image = begin(c + AHEAD, image)
    return image.reshape(1, 1, grid_n, 2 * grid_n)


def solution(mesh):
    in_specs = (
        P(("wa", "facet"), None, None),
        P(("wa", "facet"), None, None),
        P(("wa", "facet"), None),
        P(("wa", "facet"), None),
        P("facet", None, None),
    )
    out_specs = P("wa", "facet", None, None)
    return jax.shard_map(
        on_device, mesh=mesh, in_specs=in_specs, out_specs=out_specs, check_vma=False
    )
```

```python
import functools
import math

import jax
import jax.numpy as jnp
import numpy as np
from jax import lax
from jax.experimental import pallas as pl
from jax.experimental.pallas import tpu as pltpu
from jax.sharding import PartitionSpec as P

SUB = 64
LANES = 128
ROWS = 8
GROUP = 8
PARTS = (7, 7, 7, 6, 5)
EARLY = 3
AHEAD = 3
LAG = 2
DIGITS = 3
DIGIT = 16.0
SINE = tuple(
    float(v)
    for v in np.linalg.lstsq(
        *(
            lambda x, w: (
                (x[:, None] ** np.arange(1, 10, 2)[None, :]) * w[:, None],
                np.sin(2 * np.pi * x) * w,
            )
        )(
            0.5 * np.cos(np.pi * (np.arange(2000) + 0.5) / 4000),
            np.ones(2000),
        ),
        rcond=None,
    )[0]
)


def sine_turns(turns):
    x = turns - jnp.round(turns)
    x2 = x * x
    total = jnp.full_like(x, SINE[-1])
    for c in SINE[-2::-1]:
        total = total * x2 + c
    return total * x


def pack_kernel(owners, cap, routes, offsets, angles, vis, out):
    rows = routes.shape[1]
    owner = lax.broadcasted_iota(jnp.int32, (owners, rows), 0)
    named = jnp.where(owner == routes[...], 1.0, 0.0)
    before = lax.broadcasted_iota(jnp.int32, (rows, rows), 0)
    until = before <= lax.broadcasted_iota(jnp.int32, (rows, rows), 1)
    until = jnp.where(until, 1.0, 0.0).astype(jnp.bfloat16)
    tally = jnp.dot(named.astype(jnp.bfloat16), until, preferred_element_type=jnp.float32)
    rank = jnp.sum(tally * named, axis=0, keepdims=True).astype(jnp.int32) - 1
    slot = routes[...] * cap + rank
    chosen = lax.broadcasted_iota(jnp.int32, (owners * cap, rows), 0) == slot
    chosen = jnp.where(chosen, 1.0, 0.0).astype(jnp.bfloat16)

    def pick(values):
        return lax.dot_general(
            chosen, values, (((1,), (1,)), ((), ())), preferred_element_type=jnp.float32
        )

    whole = angles[...]
    high = whole.astype(jnp.bfloat16)
    whole = whole - high.astype(jnp.float32)
    middle = whole.astype(jnp.bfloat16)
    low = (whole - middle.astype(jnp.float32)).astype(jnp.bfloat16)
    spot = lax.broadcasted_iota(jnp.int32, vis.shape, 0)
    digits = jnp.where(spot == 2 * DIGITS, 1, 0)
    for axis in range(2):
        for place in range(DIGITS):
            digit = (offsets[axis : axis + 1, :] >> (3 * place)) & 7
            digits = digits + jnp.where(spot == axis * DIGITS + place, digit, 0)
    digits = (digits.astype(jnp.float32) * DIGIT).astype(jnp.bfloat16)
    out[:, 0] = ((pick(high) + pick(middle)) + pick(low)).reshape(owners, cap, LANES)
    out[:, 1] = (pick(vis[...]) + pick(digits)).reshape(owners, cap, LANES)


def pack(routes, offsets, angles, vis, owners, cap):
    vmem = pl.BlockSpec(memory_space=pltpu.VMEM)
    return pl.pallas_call(
        functools.partial(pack_kernel, owners, cap),
        out_shape=jax.ShapeDtypeStruct((owners, 2, cap, LANES), jnp.float32),
        in_specs=[vmem] * 4,
        out_specs=vmem,
        name="pack",
    )(routes, offsets, angles, vis)


def grid_kernel(
    cells, filled, got, first_hbm, second_hbm, dense, first, second,
    turns_u, turns_v, amp_a, amp_b, grid, places, sems, *stages,
):
    slots = got.shape[0] // 2
    owners = filled.shape[0]
    cap = slots // owners
    grid_n = dense.shape[0]
    blocks = grid_n // SUB
    group = stages[0].shape[0]
    bases, lefts, rights, pieces = (stages[2 * k : 2 * k + 2] for k in range(4))
    copies = [
        pltpu.make_async_copy(first_hbm, first, sems.at[0]),
        pltpu.make_async_copy(second_hbm, second, sems.at[1]),
    ]
    for copy in copies:
        copy.start()

    lane = lax.broadcasted_iota(jnp.int32, (ROWS, LANES), 1)
    low = lane < SUB
    row = lax.broadcasted_iota(jnp.int32, (ROWS, LANES), 0)
    quarter = jnp.where(low, 0.25, 0.0).astype(jnp.float32)
    sign = jnp.where(low, -1.0, 1.0).astype(jnp.float32)
    row_f = row.astype(jnp.float32)
    upper = row < ROWS // 2
    eights = ((row & (ROWS // 2 - 1)) * ROWS + ROWS).astype(jnp.float32)
    middle = SUB // ROWS // 2

    low_cap = lax.broadcasted_iota(jnp.int32, (cap, LANES), 1) < SUB

    def spread_out(i, count):
        angles = got[pl.ds(i * (2 * cap), cap), :]
        vis = got[pl.ds(i * (2 * cap) + cap, cap), :]
        vis = vis - jnp.round(vis * (1.0 / DIGIT)) * DIGIT
        rows = pl.ds(count, cap)
        both = angles * (1.0 / (2.0 * math.pi))
        swapped = pltpu.roll(both, SUB, 1)
        turns_u[rows, :] = jnp.where(low_cap, both, swapped)
        turns_v[rows, :] = jnp.where(low_cap, swapped, both)
        both = vis * (1.0 / math.sqrt(SUB))
        swapped = pltpu.roll(both, SUB, 1)
        amp_a[rows, :] = jnp.where(low_cap, both, swapped)
        amp_b[rows, :] = jnp.where(low_cap, swapped, both)
        for k in range(cap):
            places[count + k] = cells[i * cap + k]
        return count + filled[i]

    count = lax.fori_loop(0, owners, spread_out, 0, unroll=8)
    for ref in (turns_u, turns_v, amp_a, amp_b):
        ref[pl.ds(count, 2 * group), :] = jnp.zeros((2 * group, LANES), jnp.float32)
    for k in range(2 * group):
        places[count + k] = 0
    pairs = jnp.maximum((count + 2 * group - 1) // (2 * group), 1)
    groups = 2 * pairs

    def offset_of(s, axis):
        return (places[s] >> (3 * DIGITS * axis)) & ((1 << (3 * DIGITS)) - 1)

    def clear(b, _):
        grid[pl.ds(b * grid_n, grid_n), :] = jnp.zeros((grid_n, LANES), grid.dtype)
        return 0

    lax.fori_loop(0, blocks + 1, clear, 0)

    def spread(ref, s):
        return jnp.broadcast_to(ref[pl.ds(s, 1), :], (ROWS, LANES))

    def find_bases(g, out):
        for i in range(group):
            s = g * group + i
            tu, tv = spread(turns_u, s), spread(turns_v, s)
            a, b = spread(amp_a, s), spread(amp_b, s)
            cs = sine_turns(tu * row_f + quarter)
            sc = pltpu.roll(cs, SUB, 1) * sign
            out[i, 0] = cs * a + sc * b
            out[i, 1] = sc * a - cs * b
            cs = sine_turns(tv * row_f + quarter)
            out[i, 2] = -(cs * sign)
            out[i, 3] = pltpu.roll(cs, SUB, 1)
            cs = sine_turns(jnp.where(upper, tu, tv) * eights + quarter)
            sc = pltpu.roll(cs, SUB, 1)
            out[i, 4] = jnp.where(low, cs, sc)
            out[i, 5] = jnp.where(low, sc, cs)

    def find_rows(source, left, right):
        for i in range(group):

            def line(k, j):
                return jnp.broadcast_to(source[i, k, j : j + 1, :], (ROWS, LANES))

            x, y = source[i, 0], source[i, 1]
            parts = [x]
            for j in range(middle):
                along, across = x * line(4, j), y * line(5, j)
                parts = [along - across] + parts
                if j + 1 < middle:
                    parts = parts + [along + across]
            left[i] = jnp.concatenate(parts, axis=0).astype(jnp.bfloat16)

            def keep(k, value_re, value_im):
                for place in (k, 2 * middle + k):
                    right[i, 0, place * ROWS : (place + 1) * ROWS, :] = value_re
                    right[i, 1, place * ROWS : (place + 1) * ROWS, :] = value_im

            x, y = source[i, 2], source[i, 3]
            keep(middle, x, y)
            for j in range(middle):
                wr, wi = line(4, middle + j), line(5, middle + j)
                xr, xi, yr, yi = x * wr, x * wi, y * wr, y * wi
                keep(middle - 1 - j, xr + yi, yr - xi)
                if j + 1 < middle:
                    keep(middle + 1 + j, xr - yi, yr + xi)

    def multiply(g, left, right, out):
        blank = jnp.zeros((SUB, LANES), jnp.bfloat16)
        for first_i in range(0, group, 2):
            halves = []
            for i in (first_i, first_i + 1):
                shift = offset_of(g * group + i, 1) & (SUB - 1)
                rows = pl.ds(SUB - shift, SUB)
                turned = jnp.concatenate([right[i, 0, rows, :], right[i, 1, rows, :]], axis=0)
                halves.append(turned.astype(jnp.bfloat16))
            upper_rows = jnp.concatenate([left[first_i], blank], axis=1)
            lower_rows = jnp.concatenate([blank, left[first_i + 1]], axis=1)
            both = lax.dot_general(
                jnp.concatenate([upper_rows, lower_rows], axis=0),
                jnp.concatenate(halves, axis=1),
                (((1,), (1,)), ((), ())),
                preferred_element_type=jnp.float32,
            )
            out[first_i] = both[:SUB]
            out[first_i + 1] = both[SUB:]

    cell = lax.broadcasted_iota(jnp.int32, (SUB, LANES), 1) & (SUB - 1)

    def add(g, formed):
        for i in range(group):
            s = g * group + i
            off_u, off_v = offset_of(s, 0), offset_of(s, 1)
            start = (off_v >> (SUB.bit_length() - 1)) * grid_n + off_u
            here = cell >= (off_v & (SUB - 1))
            places = [grid.at[pl.ds(start + side * grid_n, SUB), :] for side in range(2)]
            totals = [place[...] + formed[i] for place in places]
            pltpu.store(places[0], totals[0], mask=here)
            pltpu.store(places[1], totals[1], mask=~here)

    pieces[0][...] = jnp.zeros_like(pieces[0])
    lefts[1][...] = jnp.zeros_like(lefts[1])
    rights[1][...] = jnp.zeros_like(rights[1])
    find_bases(0, bases[0])

    def pair(p, _):
        for k in range(2):
            g = 2 * p + k
            add(jnp.maximum(g - 2, 0), pieces[k])
            multiply(jnp.maximum(g - 1, 0), lefts[1 - k], rights[1 - k], pieces[1 - k])
            find_rows(bases[k], lefts[k], rights[k])
            find_bases(jnp.minimum(g + 1, groups - 1), bases[1 - k])
        return 0

    lax.fori_loop(0, pairs, pair, 0)
    add(groups - 2, pieces[0])
    multiply(groups - 1, lefts[1], rights[1], pieces[1])
    add(groups - 1, pieces[1])

    for b in range(blocks):
        dense[:, b * LANES : (b + 1) * LANES] = grid[b * grid_n : (b + 1) * grid_n, :].astype(jnp.bfloat16)
    for copy in copies:
        copy.wait()


def form_grid(cells, filled, got, first, second):
    slots = got.shape[0] // 2
    grid_n = first.shape[0]
    blocks = grid_n // SUB
    group = math.gcd(slots // 2, GROUP)
    smem = pl.BlockSpec(memory_space=pltpu.SMEM)
    vmem = pl.BlockSpec(memory_space=pltpu.VMEM)
    hbm = pl.BlockSpec(memory_space=pltpu.HBM)
    line = pltpu.VMEM((slots + 2 * group, LANES), jnp.float32)
    stages = [
        pltpu.VMEM((group, 6, ROWS, LANES), jnp.float32),
        pltpu.VMEM((group, SUB, LANES), jnp.bfloat16),
        pltpu.VMEM((group, 2, 2 * SUB, LANES), jnp.float32),
        pltpu.VMEM((group, SUB, LANES), jnp.float32),
    ]
    return pl.pallas_call(
        grid_kernel,
        out_shape=[
            pltpu.VMEM((grid_n, 2 * grid_n), jnp.bfloat16),
            pltpu.VMEM(first.shape, jnp.bfloat16),
            pltpu.VMEM(second.shape, jnp.bfloat16),
        ],
        in_specs=[smem, smem, vmem, hbm, hbm],
        out_specs=[vmem] * 3,
        scratch_shapes=[
            line, line, line, line,
            pltpu.VMEM(((blocks + 1) * grid_n, LANES), jnp.float32),
            pltpu.SMEM((slots + 2 * group,), jnp.int32),
            pltpu.SemaphoreType.DMA((2,)),
            *(stage for stage in stages for _ in range(2)),
        ],
        compiler_params=pltpu.CompilerParams(vmem_limit_bytes=24 * 1024 * 1024),
        name="grid",
    )(
        cells,
        filled,
        got,
        pltpu.with_memory_space_constraint(first, pltpu.HBM),
        pltpu.with_memory_space_constraint(second, pltpu.HBM),
    )


def transform_rows(dense, first, second, start, end):
    grid_n = dense.shape[0]
    rows = end - start
    both = jnp.concatenate([first[start:end, :grid_n], first[start:end, grid_n:]], axis=0)
    both = jnp.dot(both, dense[...], preferred_element_type=jnp.float32)
    sign = jnp.where(lax.broadcasted_iota(jnp.int32, (rows, LANES), 1) < SUB, -1.0, 1.0)
    half = [
        both[:rows, at : at + LANES] + pltpu.roll(both[rows:, at : at + LANES], SUB, 1) * sign
        for at in range(0, 2 * grid_n, LANES)
    ]
    half = jnp.concatenate(half, axis=1).astype(jnp.bfloat16)
    return jnp.dot(half, second[...], preferred_element_type=jnp.float32)


def sent_rows_kernel(start, end, dense, first, second, *rest):
    image, send = rest[-2:]
    rows = transform_rows(dense, first, second, start, end)
    image[start:end, :] = rows
    send[...] = rows.astype(jnp.bfloat16)


def turn_rows(phase, turns, start, end):
    grid_n = phase.shape[1]
    part = phase[start:end, :] * (1.0 / (2.0 * math.pi))
    turns[start:end, :grid_n] = sine_turns(part + 0.25)
    turns[start:end, grid_n:] = sine_turns(part)


def other_rows_kernel(bounds, done, phase, dense, first, second, _, image, turns):
    for c, (start, end) in enumerate(zip(bounds, bounds[1:])):
        turn_rows(phase, turns, start, end)
        if c >= done:
            image[start:end, :] = transform_rows(dense, first, second, start, end)


def pinned(*arrays):
    return [pltpu.with_memory_space_constraint(x, pltpu.VMEM) for x in arrays]


def sent_rows(dense, first, second, start, end, image=None):
    grid_n = first.shape[0]
    vmem = pl.BlockSpec(memory_space=pltpu.VMEM)
    operands = [dense, first, second] + ([] if image is None else [image])
    return pl.pallas_call(
        functools.partial(sent_rows_kernel, start, end),
        out_shape=[
            pltpu.VMEM((grid_n, 2 * grid_n), jnp.float32),
            pltpu.VMEM((end - start, 2 * grid_n), jnp.bfloat16),
        ],
        in_specs=[vmem] * len(operands),
        out_specs=[vmem] * 2,
        input_output_aliases={} if image is None else {3: 0},
        compiler_params=pltpu.CompilerParams(vmem_limit_bytes=8 * 1024 * 1024),
        name="sent_rows",
    )(*pinned(*operands))


def other_rows(phase, dense, first, second, image, bounds, done):
    vmem = pl.BlockSpec(memory_space=pltpu.VMEM)
    return pl.pallas_call(
        functools.partial(other_rows_kernel, bounds, done),
        out_shape=[pltpu.VMEM(image.shape, jnp.float32), pltpu.VMEM(image.shape, jnp.float32)],
        in_specs=[vmem] * 5,
        out_specs=[vmem] * 2,
        input_output_aliases={4: 0},
        compiler_params=pltpu.CompilerParams(vmem_limit_bytes=8 * 1024 * 1024),
        name="other_rows",
    )(*pinned(phase, dense, first, second, image))


def dft_tables(grid_n):
    line = np.arange(grid_n)
    angle = (line[:, None] * line[None, :] % grid_n) * (2.0 * np.pi / grid_n)
    cos = np.cos(angle) / math.sqrt(grid_n)
    sin = np.sin(angle) / math.sqrt(grid_n)
    first = np.concatenate([cos, sin], axis=1)
    real = np.concatenate([cos, sin], axis=1).reshape(grid_n // SUB, SUB, 2 * grid_n)
    imag = np.concatenate([-sin, cos], axis=1).reshape(grid_n // SUB, SUB, 2 * grid_n)
    second = np.concatenate([real, imag], axis=1).reshape(2 * grid_n, 2 * grid_n)
    return first.astype(np.float32).astype(jnp.bfloat16), second.astype(np.float32).astype(jnp.bfloat16)


def send_up(part, hop):
    return lax.ppermute(part, "wa", [(hop - 1, hop)])


def turn_and_add(hop, start, incoming, image, turns, new_image, send=None):
    grid_n = image.shape[1] // 2
    rows = pl.ds(start, incoming.shape[0])
    re_cells, im_cells = pl.ds(0, grid_n), pl.ds(grid_n, grid_n)

    @pl.when(lax.axis_index("wa") == hop)
    def _():
        re = incoming[:, re_cells].astype(jnp.float32)
        im = incoming[:, im_cells].astype(jnp.float32)
        turn_re, turn_im = turns[rows, re_cells], turns[rows, im_cells]
        new_re = turn_re * re - turn_im * im + image[rows, re_cells]
        new_im = turn_re * im + turn_im * re + image[rows, im_cells]
        new_image[rows, re_cells] = new_re
        new_image[rows, im_cells] = new_im
        if send is not None:
            send[:, re_cells] = new_re.astype(jnp.bfloat16)
            send[:, im_cells] = new_im.astype(jnp.bfloat16)


def horner_kernel(hop, start, incoming, image, turns, send, new_image):
    turn_and_add(hop, start, incoming, image, turns, new_image, send)


def horner_step(hop, start, end, incoming, image, turns):
    vmem = pl.BlockSpec(memory_space=pltpu.VMEM)
    return pl.pallas_call(
        functools.partial(horner_kernel, hop, start),
        out_shape=[
            pltpu.VMEM((end - start, image.shape[1]), jnp.bfloat16),
            pltpu.VMEM(image.shape, jnp.float32),
        ],
        in_specs=[vmem] * 3,
        out_specs=[vmem] * 2,
        input_output_aliases={1: 1},
        compiler_params=pltpu.CompilerParams(vmem_limit_bytes=4 * 1024 * 1024),
        name="horner",
    )(*pinned(incoming, image, turns))


def last_kernel(hop, start, incoming, image, turns, *rest):
    new_image, result, sem = rest[-3:]
    turn_and_add(hop, start, incoming, image, turns, new_image)
    rows = pl.ds(start, incoming.shape[0])
    copy = pltpu.make_async_copy(new_image.at[rows, :], result.at[rows, :], sem)
    copy.start()
    copy.wait()


def last_step(hop, start, end, incoming, image, turns, result):
    vmem = pl.BlockSpec(memory_space=pltpu.VMEM)
    hbm = pl.BlockSpec(memory_space=pltpu.HBM)
    known = [] if result is None else [pltpu.with_memory_space_constraint(result, pltpu.HBM)]
    return pl.pallas_call(
        functools.partial(last_kernel, hop, start),
        out_shape=[pltpu.VMEM(image.shape, jnp.float32), pltpu.HBM(image.shape, jnp.float32)],
        in_specs=[vmem] * 3 + [hbm] * len(known),
        out_specs=[vmem, hbm],
        input_output_aliases={1: 0, **({3: 1} if known else {})},
        scratch_shapes=[pltpu.SemaphoreType.DMA],
        compiler_params=pltpu.CompilerParams(vmem_limit_bytes=4 * 1024 * 1024),
        name="last",
    )(*pinned(incoming, image, turns), *known)


def begin_kernel(start, image, send, _):
    @pl.when(lax.axis_index("wa") == 0)
    def _():
        send[...] = image[pl.ds(start, send.shape[0]), :].astype(jnp.bfloat16)


def begin_chain(start, end, image):
    vmem = pl.BlockSpec(memory_space=pltpu.VMEM)
    return pl.pallas_call(
        functools.partial(begin_kernel, start),
        out_shape=[
            pltpu.VMEM((end - start, image.shape[1]), jnp.bfloat16),
            pltpu.VMEM(image.shape, jnp.float32),
        ],
        in_specs=[vmem],
        out_specs=[vmem] * 2,
        input_output_aliases={0: 1},
        compiler_params=pltpu.CompilerParams(vmem_limit_bytes=4 * 1024 * 1024),
        name="begin",
    )(*pinned(image))


def on_device(visibilities, uv_angles, routes, offsets, pixel_phase):
    sub_count = visibilities.shape[0]
    count_vis = visibilities.shape[2]
    grid_n = pixel_phase.shape[1]
    planes = lax.axis_size("wa")
    owners = planes * lax.axis_size("facet")
    cap = max(2, (2 * sub_count + owners - 1) // owners)
    slots = owners * cap
    sent = pack(
        routes.T,
        offsets.T,
        uv_angles.transpose(1, 2, 0).reshape(2 * count_vis, sub_count),
        visibilities.transpose(1, 2, 0).reshape(2 * count_vis, sub_count),
        owners,
        cap,
    ).reshape(2 * slots, LANES)
    got = lax.all_to_all(sent, ("wa", "facet"), split_axis=0, concat_axis=0, tiled=True)
    digits = got.reshape(owners, 2, cap, LANES)[:, 1, :, : 2 * DIGITS + 1]
    digits = jnp.round(digits * (1.0 / DIGIT)).astype(jnp.int32)
    filled = jnp.sum(digits[:, :, 2 * DIGITS], axis=1)
    cells = digits[:, :, 0]
    for place in range(1, 2 * DIGITS):
        cells = cells + (digits[:, :, place] << (3 * place))
    first, second = (jnp.asarray(x) for x in dft_tables(grid_n))
    dense, first, second = form_grid(cells.reshape(slots), filled, got, first, second)

    units = grid_n // 16
    bounds = [0] + [16 * (units * sum(PARTS[: i + 1]) // sum(PARTS)) for i in range(len(PARTS))]
    count = len(PARTS)
    image, result, incoming = None, None, {}
    for c in range(EARLY):
        image, send = sent_rows(dense, first, second, bounds[c], bounds[c + 1], image)
        incoming[1, c] = send_up(send, 1)
    image, turns = other_rows(pixel_phase[0], dense, first, second, image, bounds, EARLY)

    def begin(c, image):
        if c < count:
            send, image = begin_chain(bounds[c], bounds[c + 1], image)
            incoming[1, c] = send_up(send, 1)
        return image

    for c in range(EARLY, AHEAD):
        image = begin(c, image)
    for beat in range(count + LAG * planes):
        for hop in range(1, planes):
            c = beat - LAG * (hop - 1)
            if 0 <= c < count:
                rows = bounds[c], bounds[c + 1]
                if hop + 1 < planes:
                    send, image = horner_step(hop, *rows, incoming[hop, c], image, turns)
                    incoming[hop + 1, c] = send_up(send, hop + 1)
                else:
                    image, result = last_step(hop, *rows, incoming[hop, c], image, turns, result)
                if hop == 1:
                    image = begin(c + AHEAD, image)
    return result.reshape(1, 1, grid_n, 2 * grid_n)


def solution(mesh):
    in_specs = (
        P(("wa", "facet"), None, None),
        P(("wa", "facet"), None, None),
        P(("wa", "facet"), None),
        P(("wa", "facet"), None),
        P("facet", None, None),
    )
    out_specs = P("wa", "facet", None, None)
    return jax.shard_map(
        on_device, mesh=mesh, in_specs=in_specs, out_specs=out_specs, check_vma=False
    )
```

```python
import functools
import math

import jax
import jax.numpy as jnp
import numpy as np
from jax import lax
from jax.experimental import pallas as pl
from jax.experimental.pallas import tpu as pltpu
from jax.sharding import PartitionSpec as P

SUB = 64
LANES = 128
ROWS = 8
GROUP = 8
PARTS = (7, 7, 7, 6, 5)
EARLY = 3
AHEAD = 3
LAG = 2
DIGITS = 3
DIGIT = 16.0
SINE = tuple(
    float(v)
    for v in np.linalg.lstsq(
        *(
            lambda x, w: (
                (x[:, None] ** np.arange(1, 10, 2)[None, :]) * w[:, None],
                np.sin(2 * np.pi * x) * w,
            )
        )(
            0.5 * np.cos(np.pi * (np.arange(2000) + 0.5) / 4000),
            np.ones(2000),
        ),
        rcond=None,
    )[0]
)


def sine_turns(turns):
    x = turns - jnp.round(turns)
    x2 = x * x
    total = jnp.full_like(x, SINE[-1])
    for c in SINE[-2::-1]:
        total = total * x2 + c
    return total * x


def pack_kernel(owners, cap, *refs):
    sources, out, places, sems = refs[:4], refs[4], refs[5:9], refs[9]
    copies = [
        pltpu.make_async_copy(source, place, sems.at[k])
        for k, (source, place) in enumerate(zip(sources, places))
    ]
    for copy in copies:
        copy.start()
    for copy in copies:
        copy.wait()
    routes, offsets, angles, vis = places
    rows = routes.shape[1]
    owner = lax.broadcasted_iota(jnp.int32, (owners, rows), 0)
    named = jnp.where(owner == routes[...], 1.0, 0.0)
    before = lax.broadcasted_iota(jnp.int32, (rows, rows), 0)
    until = before <= lax.broadcasted_iota(jnp.int32, (rows, rows), 1)
    until = jnp.where(until, 1.0, 0.0).astype(jnp.bfloat16)
    tally = jnp.dot(named.astype(jnp.bfloat16), until, preferred_element_type=jnp.float32)
    rank = jnp.sum(tally * named, axis=0, keepdims=True).astype(jnp.int32) - 1
    slot = routes[...] * cap + rank
    chosen = lax.broadcasted_iota(jnp.int32, (owners * cap, rows), 0) == slot
    chosen = jnp.where(chosen, 1.0, 0.0).astype(jnp.bfloat16)

    def pick(values):
        return lax.dot_general(
            chosen, values, (((1,), (1,)), ((), ())), preferred_element_type=jnp.float32
        )

    whole = angles[...]
    high = whole.astype(jnp.bfloat16)
    whole = whole - high.astype(jnp.float32)
    middle = whole.astype(jnp.bfloat16)
    low = (whole - middle.astype(jnp.float32)).astype(jnp.bfloat16)
    spot = lax.broadcasted_iota(jnp.int32, vis.shape, 0)
    digits = jnp.where(spot == 2 * DIGITS, 1, 0)
    for axis in range(2):
        for place in range(DIGITS):
            digit = (offsets[axis : axis + 1, :] >> (3 * place)) & 7
            digits = digits + jnp.where(spot == axis * DIGITS + place, digit, 0)
    digits = (digits.astype(jnp.float32) * DIGIT).astype(jnp.bfloat16)
    out[:, 0] = ((pick(high) + pick(middle)) + pick(low)).reshape(owners, cap, LANES)
    out[:, 1] = (pick(vis[...]) + pick(digits)).reshape(owners, cap, LANES)


def pack(routes, offsets, angles, vis, owners, cap):
    vmem = pl.BlockSpec(memory_space=pltpu.VMEM)
    return pl.pallas_call(
        functools.partial(pack_kernel, owners, cap),
        out_shape=pltpu.VMEM((owners, 2, cap, LANES), jnp.float32),
        compiler_params=pltpu.CompilerParams(vmem_limit_bytes=8 * 1024 * 1024),
        in_specs=[pl.BlockSpec(memory_space=pltpu.HBM)] * 4,
        out_specs=vmem,
        scratch_shapes=[
            *(pltpu.VMEM(x.shape, x.dtype) for x in (routes, offsets, angles, vis)),
            pltpu.SemaphoreType.DMA((4,)),
        ],
        name="pack",
    )(*(pltpu.with_memory_space_constraint(x, pltpu.HBM) for x in (routes, offsets, angles, vis)))


def grid_kernel(
    cells, filled, got, first_hbm, second_hbm, dense, first, second,
    turns_u, turns_v, amp_a, amp_b, grid, places, sems, *stages,
):
    slots = got.shape[0] // 2
    owners = filled.shape[0]
    cap = slots // owners
    grid_n = dense.shape[0]
    blocks = grid_n // SUB
    group = stages[0].shape[0]
    bases, lefts, rights, pieces = (stages[2 * k : 2 * k + 2] for k in range(4))
    copies = [
        pltpu.make_async_copy(first_hbm, first, sems.at[0]),
        pltpu.make_async_copy(second_hbm, second, sems.at[1]),
    ]
    for copy in copies:
        copy.start()

    lane = lax.broadcasted_iota(jnp.int32, (ROWS, LANES), 1)
    low = lane < SUB
    row = lax.broadcasted_iota(jnp.int32, (ROWS, LANES), 0)
    quarter = jnp.where(low, 0.25, 0.0).astype(jnp.float32)
    sign = jnp.where(low, -1.0, 1.0).astype(jnp.float32)
    row_f = row.astype(jnp.float32)
    upper = row < ROWS // 2
    eights = ((row & (ROWS // 2 - 1)) * ROWS + ROWS).astype(jnp.float32)
    middle = SUB // ROWS // 2

    low_cap = lax.broadcasted_iota(jnp.int32, (cap, LANES), 1) < SUB

    def spread_out(i, count):
        angles = got[pl.ds(i * (2 * cap), cap), :]
        vis = got[pl.ds(i * (2 * cap) + cap, cap), :]
        vis = vis - jnp.round(vis * (1.0 / DIGIT)) * DIGIT
        rows = pl.ds(count, cap)
        both = angles * (1.0 / (2.0 * math.pi))
        swapped = pltpu.roll(both, SUB, 1)
        turns_u[rows, :] = jnp.where(low_cap, both, swapped)
        turns_v[rows, :] = jnp.where(low_cap, swapped, both)
        both = vis * (1.0 / math.sqrt(SUB))
        swapped = pltpu.roll(both, SUB, 1)
        amp_a[rows, :] = jnp.where(low_cap, both, swapped)
        amp_b[rows, :] = jnp.where(low_cap, swapped, both)
        for k in range(cap):
            places[count + k] = cells[i * cap + k]
        return count + filled[i]

    count = lax.fori_loop(0, owners, spread_out, 0, unroll=8)
    for ref in (turns_u, turns_v, amp_a, amp_b):
        ref[pl.ds(count, 2 * group), :] = jnp.zeros((2 * group, LANES), jnp.float32)
    for k in range(2 * group):
        places[count + k] = 0
    pairs = jnp.maximum((count + 2 * group - 1) // (2 * group), 1)
    groups = 2 * pairs

    def offset_of(s, axis):
        return (places[s] >> (3 * DIGITS * axis)) & ((1 << (3 * DIGITS)) - 1)

    def clear(b, _):
        grid[pl.ds(b * grid_n, grid_n), :] = jnp.zeros((grid_n, LANES), grid.dtype)
        return 0

    lax.fori_loop(0, blocks + 1, clear, 0)

    def spread(ref, s):
        return jnp.broadcast_to(ref[pl.ds(s, 1), :], (ROWS, LANES))

    def find_bases(g, out):
        for i in range(group):
            s = g * group + i
            tu, tv = spread(turns_u, s), spread(turns_v, s)
            a, b = spread(amp_a, s), spread(amp_b, s)
            cs = sine_turns(tu * row_f + quarter)
            sc = pltpu.roll(cs, SUB, 1) * sign
            out[i, 0] = cs * a + sc * b
            out[i, 1] = sc * a - cs * b
            cs = sine_turns(tv * row_f + quarter)
            out[i, 2] = -(cs * sign)
            out[i, 3] = pltpu.roll(cs, SUB, 1)
            cs = sine_turns(jnp.where(upper, tu, tv) * eights + quarter)
            sc = pltpu.roll(cs, SUB, 1)
            out[i, 4] = jnp.where(low, cs, sc)
            out[i, 5] = jnp.where(low, sc, cs)

    def find_rows(source, left, right):
        for i in range(group):

            def line(k, j):
                return jnp.broadcast_to(source[i, k, j : j + 1, :], (ROWS, LANES))

            x, y = source[i, 0], source[i, 1]
            parts = [x]
            for j in range(middle):
                along, across = x * line(4, j), y * line(5, j)
                parts = [along - across] + parts
                if j + 1 < middle:
                    parts = parts + [along + across]
            left[i] = jnp.concatenate(parts, axis=0).astype(jnp.bfloat16)

            def keep(k, value_re, value_im):
                for place in (k, 2 * middle + k):
                    right[i, 0, place * ROWS : (place + 1) * ROWS, :] = value_re
                    right[i, 1, place * ROWS : (place + 1) * ROWS, :] = value_im

            x, y = source[i, 2], source[i, 3]
            keep(middle, x, y)
            for j in range(middle):
                wr, wi = line(4, middle + j), line(5, middle + j)
                xr, xi, yr, yi = x * wr, x * wi, y * wr, y * wi
                keep(middle - 1 - j, xr + yi, yr - xi)
                if j + 1 < middle:
                    keep(middle + 1 + j, xr - yi, yr + xi)

    def multiply(g, left, right, out):
        blank = jnp.zeros((SUB, LANES), jnp.bfloat16)
        for first_i in range(0, group, 2):
            halves = []
            for i in (first_i, first_i + 1):
                shift = offset_of(g * group + i, 1) & (SUB - 1)
                rows = pl.ds(SUB - shift, SUB)
                turned = jnp.concatenate([right[i, 0, rows, :], right[i, 1, rows, :]], axis=0)
                halves.append(turned.astype(jnp.bfloat16))
            upper_rows = jnp.concatenate([left[first_i], blank], axis=1)
            lower_rows = jnp.concatenate([blank, left[first_i + 1]], axis=1)
            both = lax.dot_general(
                jnp.concatenate([upper_rows, lower_rows], axis=0),
                jnp.concatenate(halves, axis=1),
                (((1,), (1,)), ((), ())),
                preferred_element_type=jnp.float32,
            )
            out[first_i] = both[:SUB]
            out[first_i + 1] = both[SUB:]

    cell = lax.broadcasted_iota(jnp.int32, (SUB, LANES), 1) & (SUB - 1)

    def add(g, formed):
        for i in range(group):
            s = g * group + i
            off_u, off_v = offset_of(s, 0), offset_of(s, 1)
            start = (off_v >> (SUB.bit_length() - 1)) * grid_n + off_u
            here = cell >= (off_v & (SUB - 1))
            places = [grid.at[pl.ds(start + side * grid_n, SUB), :] for side in range(2)]
            totals = [place[...] + formed[i] for place in places]
            pltpu.store(places[0], totals[0], mask=here)
            pltpu.store(places[1], totals[1], mask=~here)

    pieces[0][...] = jnp.zeros_like(pieces[0])
    lefts[1][...] = jnp.zeros_like(lefts[1])
    rights[1][...] = jnp.zeros_like(rights[1])
    find_bases(0, bases[0])

    def pair(p, _):
        for k in range(2):
            g = 2 * p + k
            add(jnp.maximum(g - 2, 0), pieces[k])
            multiply(jnp.maximum(g - 1, 0), lefts[1 - k], rights[1 - k], pieces[1 - k])
            find_rows(bases[k], lefts[k], rights[k])
            find_bases(jnp.minimum(g + 1, groups - 1), bases[1 - k])
        return 0

    lax.fori_loop(0, pairs, pair, 0)
    add(groups - 2, pieces[0])
    multiply(groups - 1, lefts[1], rights[1], pieces[1])
    add(groups - 1, pieces[1])

    for b in range(blocks):
        dense[:, b * LANES : (b + 1) * LANES] = grid[b * grid_n : (b + 1) * grid_n, :].astype(jnp.bfloat16)
    for copy in copies:
        copy.wait()


def form_grid(cells, filled, got, first, second):
    slots = got.shape[0] // 2
    grid_n = first.shape[0]
    blocks = grid_n // SUB
    group = math.gcd(slots // 2, GROUP)
    smem = pl.BlockSpec(memory_space=pltpu.SMEM)
    vmem = pl.BlockSpec(memory_space=pltpu.VMEM)
    hbm = pl.BlockSpec(memory_space=pltpu.HBM)
    line = pltpu.VMEM((slots + 2 * group, LANES), jnp.float32)
    stages = [
        pltpu.VMEM((group, 6, ROWS, LANES), jnp.float32),
        pltpu.VMEM((group, SUB, LANES), jnp.bfloat16),
        pltpu.VMEM((group, 2, 2 * SUB, LANES), jnp.float32),
        pltpu.VMEM((group, SUB, LANES), jnp.float32),
    ]
    return pl.pallas_call(
        grid_kernel,
        out_shape=[
            pltpu.VMEM((grid_n, 2 * grid_n), jnp.bfloat16),
            pltpu.VMEM(first.shape, jnp.bfloat16),
            pltpu.VMEM(second.shape, jnp.bfloat16),
        ],
        in_specs=[smem, smem, vmem, hbm, hbm],
        out_specs=[vmem] * 3,
        scratch_shapes=[
            line, line, line, line,
            pltpu.VMEM(((blocks + 1) * grid_n, LANES), jnp.float32),
            pltpu.SMEM((slots + 2 * group,), jnp.int32),
            pltpu.SemaphoreType.DMA((2,)),
            *(stage for stage in stages for _ in range(2)),
        ],
        compiler_params=pltpu.CompilerParams(vmem_limit_bytes=24 * 1024 * 1024),
        name="grid",
    )(
        cells,
        filled,
        got,
        pltpu.with_memory_space_constraint(first, pltpu.HBM),
        pltpu.with_memory_space_constraint(second, pltpu.HBM),
    )


def transform_rows(dense, first, second, start, end):
    grid_n = dense.shape[0]
    rows = end - start
    both = jnp.concatenate([first[start:end, :grid_n], first[start:end, grid_n:]], axis=0)
    both = jnp.dot(both, dense[...], preferred_element_type=jnp.float32)
    sign = jnp.where(lax.broadcasted_iota(jnp.int32, (rows, LANES), 1) < SUB, -1.0, 1.0)
    half = [
        both[:rows, at : at + LANES] + pltpu.roll(both[rows:, at : at + LANES], SUB, 1) * sign
        for at in range(0, 2 * grid_n, LANES)
    ]
    half = jnp.concatenate(half, axis=1).astype(jnp.bfloat16)
    return jnp.dot(half, second[...], preferred_element_type=jnp.float32)


def sent_rows_kernel(start, end, dense, first, second, *rest):
    image, send = rest[-2:]
    rows = transform_rows(dense, first, second, start, end)
    image[start:end, :] = rows
    send[...] = rows.astype(jnp.bfloat16)


def turn_rows(phase, turns, start, end):
    grid_n = phase.shape[1]
    part = phase[start:end, :] * (1.0 / (2.0 * math.pi))
    turns[start:end, :grid_n] = sine_turns(part + 0.25)
    turns[start:end, grid_n:] = sine_turns(part)


def other_rows_kernel(bounds, done, phase, dense, first, second, _, image, turns):
    for c, (start, end) in enumerate(zip(bounds, bounds[1:])):
        turn_rows(phase, turns, start, end)
        if c >= done:
            image[start:end, :] = transform_rows(dense, first, second, start, end)


def pinned(*arrays):
    return [pltpu.with_memory_space_constraint(x, pltpu.VMEM) for x in arrays]


def sent_rows(dense, first, second, start, end, image=None):
    grid_n = first.shape[0]
    vmem = pl.BlockSpec(memory_space=pltpu.VMEM)
    operands = [dense, first, second] + ([] if image is None else [image])
    return pl.pallas_call(
        functools.partial(sent_rows_kernel, start, end),
        out_shape=[
            pltpu.VMEM((grid_n, 2 * grid_n), jnp.float32),
            pltpu.VMEM((end - start, 2 * grid_n), jnp.bfloat16),
        ],
        in_specs=[vmem] * len(operands),
        out_specs=[vmem] * 2,
        input_output_aliases={} if image is None else {3: 0},
        compiler_params=pltpu.CompilerParams(vmem_limit_bytes=8 * 1024 * 1024),
        name="sent_rows",
    )(*pinned(*operands))


def other_rows(phase, dense, first, second, image, bounds, done):
    vmem = pl.BlockSpec(memory_space=pltpu.VMEM)
    return pl.pallas_call(
        functools.partial(other_rows_kernel, bounds, done),
        out_shape=[pltpu.VMEM(image.shape, jnp.float32), pltpu.VMEM(image.shape, jnp.float32)],
        in_specs=[vmem] * 5,
        out_specs=[vmem] * 2,
        input_output_aliases={4: 0},
        compiler_params=pltpu.CompilerParams(vmem_limit_bytes=8 * 1024 * 1024),
        name="other_rows",
    )(*pinned(phase, dense, first, second, image))


def dft_tables(grid_n):
    line = np.arange(grid_n)
    angle = (line[:, None] * line[None, :] % grid_n) * (2.0 * np.pi / grid_n)
    cos = np.cos(angle) / math.sqrt(grid_n)
    sin = np.sin(angle) / math.sqrt(grid_n)
    first = np.concatenate([cos, sin], axis=1)
    real = np.concatenate([cos, sin], axis=1).reshape(grid_n // SUB, SUB, 2 * grid_n)
    imag = np.concatenate([-sin, cos], axis=1).reshape(grid_n // SUB, SUB, 2 * grid_n)
    second = np.concatenate([real, imag], axis=1).reshape(2 * grid_n, 2 * grid_n)
    return first.astype(np.float32).astype(jnp.bfloat16), second.astype(np.float32).astype(jnp.bfloat16)


def send_up(part, hop):
    return lax.ppermute(part, "wa", [(hop - 1, hop)])


def turn_and_add(hop, start, incoming, image, turns, new_image, send=None):
    grid_n = image.shape[1] // 2
    rows = pl.ds(start, incoming.shape[0])
    re_cells, im_cells = pl.ds(0, grid_n), pl.ds(grid_n, grid_n)

    @pl.when(lax.axis_index("wa") == hop)
    def _():
        re = incoming[:, re_cells].astype(jnp.float32)
        im = incoming[:, im_cells].astype(jnp.float32)
        turn_re, turn_im = turns[rows, re_cells], turns[rows, im_cells]
        new_re = turn_re * re - turn_im * im + image[rows, re_cells]
        new_im = turn_re * im + turn_im * re + image[rows, im_cells]
        new_image[rows, re_cells] = new_re
        new_image[rows, im_cells] = new_im
        if send is not None:
            send[:, re_cells] = new_re.astype(jnp.bfloat16)
            send[:, im_cells] = new_im.astype(jnp.bfloat16)


def horner_kernel(hop, start, incoming, image, turns, send, new_image):
    turn_and_add(hop, start, incoming, image, turns, new_image, send)


def horner_step(hop, start, end, incoming, image, turns):
    vmem = pl.BlockSpec(memory_space=pltpu.VMEM)
    return pl.pallas_call(
        functools.partial(horner_kernel, hop, start),
        out_shape=[
            pltpu.VMEM((end - start, image.shape[1]), jnp.bfloat16),
            pltpu.VMEM(image.shape, jnp.float32),
        ],
        in_specs=[vmem] * 3,
        out_specs=[vmem] * 2,
        input_output_aliases={1: 1},
        compiler_params=pltpu.CompilerParams(vmem_limit_bytes=4 * 1024 * 1024),
        name="horner",
    )(*pinned(incoming, image, turns))


def last_kernel(hop, start, incoming, image, turns, *rest):
    new_image, result, sem = rest[-3:]
    turn_and_add(hop, start, incoming, image, turns, new_image)
    rows = pl.ds(start, incoming.shape[0])
    copy = pltpu.make_async_copy(new_image.at[rows, :], result.at[rows, :], sem)
    copy.start()
    copy.wait()


def last_step(hop, start, end, incoming, image, turns, result):
    vmem = pl.BlockSpec(memory_space=pltpu.VMEM)
    hbm = pl.BlockSpec(memory_space=pltpu.HBM)
    known = [] if result is None else [pltpu.with_memory_space_constraint(result, pltpu.HBM)]
    return pl.pallas_call(
        functools.partial(last_kernel, hop, start),
        out_shape=[pltpu.VMEM(image.shape, jnp.float32), pltpu.HBM(image.shape, jnp.float32)],
        in_specs=[vmem] * 3 + [hbm] * len(known),
        out_specs=[vmem, hbm],
        input_output_aliases={1: 0, **({3: 1} if known else {})},
        scratch_shapes=[pltpu.SemaphoreType.DMA],
        compiler_params=pltpu.CompilerParams(vmem_limit_bytes=4 * 1024 * 1024),
        name="last",
    )(*pinned(incoming, image, turns), *known)


def begin_kernel(start, image, send, _):
    @pl.when(lax.axis_index("wa") == 0)
    def _():
        send[...] = image[pl.ds(start, send.shape[0]), :].astype(jnp.bfloat16)


def begin_chain(start, end, image):
    vmem = pl.BlockSpec(memory_space=pltpu.VMEM)
    return pl.pallas_call(
        functools.partial(begin_kernel, start),
        out_shape=[
            pltpu.VMEM((end - start, image.shape[1]), jnp.bfloat16),
            pltpu.VMEM(image.shape, jnp.float32),
        ],
        in_specs=[vmem],
        out_specs=[vmem] * 2,
        input_output_aliases={0: 1},
        compiler_params=pltpu.CompilerParams(vmem_limit_bytes=4 * 1024 * 1024),
        name="begin",
    )(*pinned(image))


def on_device(visibilities, uv_angles, routes, offsets, pixel_phase):
    sub_count = visibilities.shape[0]
    count_vis = visibilities.shape[2]
    grid_n = pixel_phase.shape[1]
    planes = lax.axis_size("wa")
    owners = planes * lax.axis_size("facet")
    cap = max(2, (2 * sub_count + owners - 1) // owners)
    slots = owners * cap
    sent = pack(
        routes.T,
        offsets.T,
        uv_angles.transpose(1, 2, 0).reshape(2 * count_vis, sub_count),
        visibilities.transpose(1, 2, 0).reshape(2 * count_vis, sub_count),
        owners,
        cap,
    ).reshape(2 * slots, LANES)
    got = lax.all_to_all(sent, ("wa", "facet"), split_axis=0, concat_axis=0, tiled=True)
    digits = got.reshape(owners, 2, cap, LANES)[:, 1, :, : 2 * DIGITS + 1]
    digits = jnp.round(digits * (1.0 / DIGIT)).astype(jnp.int32)
    filled = jnp.sum(digits[:, :, 2 * DIGITS], axis=1)
    cells = digits[:, :, 0]
    for place in range(1, 2 * DIGITS):
        cells = cells + (digits[:, :, place] << (3 * place))
    first, second = (jnp.asarray(x) for x in dft_tables(grid_n))
    dense, first, second = form_grid(cells.reshape(slots), filled, got, first, second)

    units = grid_n // 16
    bounds = [0] + [16 * (units * sum(PARTS[: i + 1]) // sum(PARTS)) for i in range(len(PARTS))]
    count = len(PARTS)
    image, result, incoming = None, None, {}
    for c in range(EARLY):
        image, send = sent_rows(dense, first, second, bounds[c], bounds[c + 1], image)
        incoming[1, c] = send_up(send, 1)
    image, turns = other_rows(pixel_phase[0], dense, first, second, image, bounds, EARLY)

    def begin(c, image):
        if c < count:
            send, image = begin_chain(bounds[c], bounds[c + 1], image)
            incoming[1, c] = send_up(send, 1)
        return image

    for c in range(EARLY, AHEAD):
        image = begin(c, image)
    for beat in range(count + LAG * planes):
        for hop in range(1, planes):
            c = beat - LAG * (hop - 1)
            if 0 <= c < count:
                rows = bounds[c], bounds[c + 1]
                if hop + 1 < planes:
                    send, image = horner_step(hop, *rows, incoming[hop, c], image, turns)
                    incoming[hop + 1, c] = send_up(send, hop + 1)
                else:
                    image, result = last_step(hop, *rows, incoming[hop, c], image, turns, result)
                if hop == 1:
                    image = begin(c + AHEAD, image)
    return result.reshape(1, 1, grid_n, 2 * grid_n)


def solution(mesh):
    in_specs = (
        P(("wa", "facet"), None, None),
        P(("wa", "facet"), None, None),
        P(("wa", "facet"), None),
        P(("wa", "facet"), None),
        P("facet", None, None),
    )
    out_specs = P("wa", "facet", None, None)
    return jax.shard_map(
        on_device, mesh=mesh, in_specs=in_specs, out_specs=out_specs, check_vma=False
    )
```

```python
import functools
import math

import jax
import jax.numpy as jnp
import numpy as np
from jax import lax
from jax.experimental import pallas as pl
from jax.experimental.pallas import tpu as pltpu
from jax.sharding import PartitionSpec as P

SUB = 64
LANES = 128
ROWS = 8
GROUP = 8
PARTS = (7, 7, 7, 7, 4)
EARLY = 3
AHEAD = 3
LAG = 2
DIGITS = 3
DIGIT = 16.0
SINE = tuple(
    float(v)
    for v in np.linalg.lstsq(
        *(
            lambda x, w: (
                (x[:, None] ** np.arange(1, 10, 2)[None, :]) * w[:, None],
                np.sin(2 * np.pi * x) * w,
            )
        )(
            0.5 * np.cos(np.pi * (np.arange(2000) + 0.5) / 4000),
            np.ones(2000),
        ),
        rcond=None,
    )[0]
)


def sine_turns(turns):
    x = turns - jnp.round(turns)
    x2 = x * x
    total = jnp.full_like(x, SINE[-1])
    for c in SINE[-2::-1]:
        total = total * x2 + c
    return total * x


def pack_kernel(owners, cap, *refs):
    sources, out, places, sems = refs[:4], refs[4], refs[5:9], refs[9]
    copies = [
        pltpu.make_async_copy(source, place, sems.at[k])
        for k, (source, place) in enumerate(zip(sources, places))
    ]
    for copy in copies:
        copy.start()
    for copy in copies:
        copy.wait()
    routes, offsets, angles, vis = places
    rows = routes.shape[1]
    owner = lax.broadcasted_iota(jnp.int32, (owners, rows), 0)
    named = jnp.where(owner == routes[...], 1.0, 0.0)
    before = lax.broadcasted_iota(jnp.int32, (rows, rows), 0)
    until = before <= lax.broadcasted_iota(jnp.int32, (rows, rows), 1)
    until = jnp.where(until, 1.0, 0.0).astype(jnp.bfloat16)
    tally = jnp.dot(named.astype(jnp.bfloat16), until, preferred_element_type=jnp.float32)
    rank = jnp.sum(tally * named, axis=0, keepdims=True).astype(jnp.int32) - 1
    slot = routes[...] * cap + rank
    chosen = lax.broadcasted_iota(jnp.int32, (owners * cap, rows), 0) == slot
    chosen = jnp.where(chosen, 1.0, 0.0).astype(jnp.bfloat16)

    def pick(values):
        return lax.dot_general(
            chosen, values, (((1,), (1,)), ((), ())), preferred_element_type=jnp.float32
        )

    whole = angles[...]
    high = whole.astype(jnp.bfloat16)
    whole = whole - high.astype(jnp.float32)
    middle = whole.astype(jnp.bfloat16)
    low = (whole - middle.astype(jnp.float32)).astype(jnp.bfloat16)
    spot = lax.broadcasted_iota(jnp.int32, vis.shape, 0)
    digits = jnp.where(spot == 2 * DIGITS, 1, 0)
    for axis in range(2):
        for place in range(DIGITS):
            digit = (offsets[axis : axis + 1, :] >> (3 * place)) & 7
            digits = digits + jnp.where(spot == axis * DIGITS + place, digit, 0)
    digits = (digits.astype(jnp.float32) * DIGIT).astype(jnp.bfloat16)
    out[:, 0] = ((pick(high) + pick(middle)) + pick(low)).reshape(owners, cap, LANES)
    out[:, 1] = (pick(vis[...]) + pick(digits)).reshape(owners, cap, LANES)


def pack(routes, offsets, angles, vis, owners, cap):
    vmem = pl.BlockSpec(memory_space=pltpu.VMEM)
    return pl.pallas_call(
        functools.partial(pack_kernel, owners, cap),
        out_shape=pltpu.VMEM((owners, 2, cap, LANES), jnp.float32),
        compiler_params=pltpu.CompilerParams(vmem_limit_bytes=8 * 1024 * 1024),
        in_specs=[pl.BlockSpec(memory_space=pltpu.HBM)] * 4,
        out_specs=vmem,
        scratch_shapes=[
            *(pltpu.VMEM(x.shape, x.dtype) for x in (routes, offsets, angles, vis)),
            pltpu.SemaphoreType.DMA((4,)),
        ],
        name="pack",
    )(*(pltpu.with_memory_space_constraint(x, pltpu.HBM) for x in (routes, offsets, angles, vis)))


def grid_kernel(
    cap, cells, got, first_hbm, second_hbm, dense, first, second,
    turns_u, turns_v, amp_a, amp_b, grid, places, sems, *stages,
):
    slots = got.shape[0] // 2
    owners = slots // cap
    grid_n = dense.shape[0]
    blocks = grid_n // SUB
    group = stages[0].shape[0]
    bases, lefts, rights, pieces = (stages[2 * k : 2 * k + 2] for k in range(4))
    copies = [
        pltpu.make_async_copy(first_hbm, first, sems.at[0]),
        pltpu.make_async_copy(second_hbm, second, sems.at[1]),
    ]
    for copy in copies:
        copy.start()

    lane = lax.broadcasted_iota(jnp.int32, (ROWS, LANES), 1)
    low = lane < SUB
    row = lax.broadcasted_iota(jnp.int32, (ROWS, LANES), 0)
    quarter = jnp.where(low, 0.25, 0.0).astype(jnp.float32)
    sign = jnp.where(low, -1.0, 1.0).astype(jnp.float32)
    row_f = row.astype(jnp.float32)
    upper = row < ROWS // 2
    eights = ((row & (ROWS // 2 - 1)) * ROWS + ROWS).astype(jnp.float32)
    middle = SUB // ROWS // 2

    low_cap = lax.broadcasted_iota(jnp.int32, (cap, LANES), 1) < SUB

    def spread_out(i, count):
        angles = got[pl.ds(i * (2 * cap), cap), :]
        vis = got[pl.ds(i * (2 * cap) + cap, cap), :]
        vis = vis - jnp.round(vis * (1.0 / DIGIT)) * DIGIT
        rows = pl.ds(count, cap)
        both = angles * (1.0 / (2.0 * math.pi))
        swapped = pltpu.roll(both, SUB, 1)
        turns_u[rows, :] = jnp.where(low_cap, both, swapped)
        turns_v[rows, :] = jnp.where(low_cap, swapped, both)
        both = vis * (1.0 / math.sqrt(SUB))
        swapped = pltpu.roll(both, SUB, 1)
        amp_a[rows, :] = jnp.where(low_cap, both, swapped)
        amp_b[rows, :] = jnp.where(low_cap, swapped, both)
        for k in range(cap):
            places[count + k] = cells[i * cap + k]
        return count + cells[slots + i]

    count = lax.fori_loop(0, owners, spread_out, 0, unroll=8)
    for ref in (turns_u, turns_v, amp_a, amp_b):
        ref[pl.ds(count, 2 * group), :] = jnp.zeros((2 * group, LANES), jnp.float32)
    for k in range(2 * group):
        places[count + k] = 0
    pairs = jnp.maximum((count + 2 * group - 1) // (2 * group), 1)
    groups = 2 * pairs

    def offset_of(s, axis):
        return (places[s] >> (3 * DIGITS * axis)) & ((1 << (3 * DIGITS)) - 1)

    def clear(b, _):
        grid[pl.ds(b * grid_n, grid_n), :] = jnp.zeros((grid_n, LANES), grid.dtype)
        return 0

    lax.fori_loop(0, blocks + 1, clear, 0)

    def spread(ref, s):
        return jnp.broadcast_to(ref[pl.ds(s, 1), :], (ROWS, LANES))

    def find_bases(g, out):
        for i in range(group):
            s = g * group + i
            tu, tv = spread(turns_u, s), spread(turns_v, s)
            a, b = spread(amp_a, s), spread(amp_b, s)
            cs = sine_turns(tu * row_f + quarter)
            sc = pltpu.roll(cs, SUB, 1) * sign
            out[i, 0] = cs * a + sc * b
            out[i, 1] = sc * a - cs * b
            cs = sine_turns(tv * row_f + quarter)
            out[i, 2] = -(cs * sign)
            out[i, 3] = pltpu.roll(cs, SUB, 1)
            cs = sine_turns(jnp.where(upper, tu, tv) * eights + quarter)
            sc = pltpu.roll(cs, SUB, 1)
            out[i, 4] = jnp.where(low, cs, sc)
            out[i, 5] = jnp.where(low, sc, cs)

    def find_rows(source, left, right):
        for i in range(group):

            def line(k, j):
                return jnp.broadcast_to(source[i, k, j : j + 1, :], (ROWS, LANES))

            x, y = source[i, 0], source[i, 1]
            parts = [x]
            for j in range(middle):
                along, across = x * line(4, j), y * line(5, j)
                parts = [along - across] + parts
                if j + 1 < middle:
                    parts = parts + [along + across]
            left[i] = jnp.concatenate(parts, axis=0).astype(jnp.bfloat16)

            def keep(k, value_re, value_im):
                for place in (k, 2 * middle + k):
                    right[i, 0, place * ROWS : (place + 1) * ROWS, :] = value_re
                    right[i, 1, place * ROWS : (place + 1) * ROWS, :] = value_im

            x, y = source[i, 2], source[i, 3]
            keep(middle, x, y)
            for j in range(middle):
                wr, wi = line(4, middle + j), line(5, middle + j)
                xr, xi, yr, yi = x * wr, x * wi, y * wr, y * wi
                keep(middle - 1 - j, xr + yi, yr - xi)
                if j + 1 < middle:
                    keep(middle + 1 + j, xr - yi, yr + xi)

    def multiply(g, left, right, out):
        blank = jnp.zeros((SUB, LANES), jnp.bfloat16)
        for first_i in range(0, group, 2):
            halves = []
            for i in (first_i, first_i + 1):
                shift = offset_of(g * group + i, 1) & (SUB - 1)
                rows = pl.ds(SUB - shift, SUB)
                turned = jnp.concatenate([right[i, 0, rows, :], right[i, 1, rows, :]], axis=0)
                halves.append(turned.astype(jnp.bfloat16))
            upper_rows = jnp.concatenate([left[first_i], blank], axis=1)
            lower_rows = jnp.concatenate([blank, left[first_i + 1]], axis=1)
            both = lax.dot_general(
                jnp.concatenate([upper_rows, lower_rows], axis=0),
                jnp.concatenate(halves, axis=1),
                (((1,), (1,)), ((), ())),
                preferred_element_type=jnp.float32,
            )
            out[first_i] = both[:SUB]
            out[first_i + 1] = both[SUB:]

    cell = lax.broadcasted_iota(jnp.int32, (SUB, LANES), 1) & (SUB - 1)

    def add(g, formed):
        for i in range(group):
            s = g * group + i
            off_u, off_v = offset_of(s, 0), offset_of(s, 1)
            start = (off_v >> (SUB.bit_length() - 1)) * grid_n + off_u
            here = cell >= (off_v & (SUB - 1))
            places = [grid.at[pl.ds(start + side * grid_n, SUB), :] for side in range(2)]
            totals = [place[...] + formed[i] for place in places]
            pltpu.store(places[0], totals[0], mask=here)
            pltpu.store(places[1], totals[1], mask=~here)

    pieces[0][...] = jnp.zeros_like(pieces[0])
    lefts[1][...] = jnp.zeros_like(lefts[1])
    rights[1][...] = jnp.zeros_like(rights[1])
    find_bases(0, bases[0])

    def pair(p, _):
        for k in range(2):
            g = 2 * p + k
            add(jnp.maximum(g - 2, 0), pieces[k])
            multiply(jnp.maximum(g - 1, 0), lefts[1 - k], rights[1 - k], pieces[1 - k])
            find_rows(bases[k], lefts[k], rights[k])
            find_bases(jnp.minimum(g + 1, groups - 1), bases[1 - k])
        return 0

    lax.fori_loop(0, pairs, pair, 0)
    add(groups - 2, pieces[0])
    multiply(groups - 1, lefts[1], rights[1], pieces[1])
    add(groups - 1, pieces[1])

    for b in range(blocks):
        dense[:, b * LANES : (b + 1) * LANES] = grid[b * grid_n : (b + 1) * grid_n, :].astype(jnp.bfloat16)
    for copy in copies:
        copy.wait()


def form_grid(cells, got, first, second, cap):
    slots = got.shape[0] // 2
    grid_n = first.shape[0]
    blocks = grid_n // SUB
    group = math.gcd(slots // 2, GROUP)
    smem = pl.BlockSpec(memory_space=pltpu.SMEM)
    vmem = pl.BlockSpec(memory_space=pltpu.VMEM)
    hbm = pl.BlockSpec(memory_space=pltpu.HBM)
    line = pltpu.VMEM((slots + 2 * group, LANES), jnp.float32)
    stages = [
        pltpu.VMEM((group, 6, ROWS, LANES), jnp.float32),
        pltpu.VMEM((group, SUB, LANES), jnp.bfloat16),
        pltpu.VMEM((group, 2, 2 * SUB, LANES), jnp.float32),
        pltpu.VMEM((group, SUB, LANES), jnp.float32),
    ]
    return pl.pallas_call(
        functools.partial(grid_kernel, cap),
        out_shape=[
            pltpu.VMEM((grid_n, 2 * grid_n), jnp.bfloat16),
            pltpu.VMEM(first.shape, jnp.bfloat16),
            pltpu.VMEM(second.shape, jnp.bfloat16),
        ],
        in_specs=[smem, vmem, hbm, hbm],
        out_specs=[vmem] * 3,
        scratch_shapes=[
            line, line, line, line,
            pltpu.VMEM(((blocks + 1) * grid_n, LANES), jnp.float32),
            pltpu.SMEM((slots + 2 * group,), jnp.int32),
            pltpu.SemaphoreType.DMA((2,)),
            *(stage for stage in stages for _ in range(2)),
        ],
        compiler_params=pltpu.CompilerParams(vmem_limit_bytes=24 * 1024 * 1024),
        name="grid",
    )(
        cells,
        got,
        pltpu.with_memory_space_constraint(first, pltpu.HBM),
        pltpu.with_memory_space_constraint(second, pltpu.HBM),
    )


def transform_rows(dense, first, second, start, end):
    grid_n = dense.shape[0]
    rows = end - start
    both = jnp.concatenate([first[start:end, :grid_n], first[start:end, grid_n:]], axis=0)
    both = jnp.dot(both, dense[...], preferred_element_type=jnp.float32)
    sign = jnp.where(lax.broadcasted_iota(jnp.int32, (rows, LANES), 1) < SUB, -1.0, 1.0)
    half = [
        both[:rows, at : at + LANES] + pltpu.roll(both[rows:, at : at + LANES], SUB, 1) * sign
        for at in range(0, 2 * grid_n, LANES)
    ]
    half = jnp.concatenate(half, axis=1).astype(jnp.bfloat16)
    return jnp.dot(half, second[...], preferred_element_type=jnp.float32)


def sent_rows_kernel(start, end, dense, first, second, *rest):
    image, send = rest[-2:]
    rows = transform_rows(dense, first, second, start, end)
    image[start:end, :] = rows
    send[...] = rows.astype(jnp.bfloat16)


def turn_rows(phase, turns, start, end):
    grid_n = phase.shape[1]
    part = phase[start:end, :] * (1.0 / (2.0 * math.pi))
    turns[start:end, :grid_n] = sine_turns(part + 0.25)
    turns[start:end, grid_n:] = sine_turns(part)


def other_rows_kernel(bounds, done, phase, dense, first, second, _, image, turns):
    for c, (start, end) in enumerate(zip(bounds, bounds[1:])):
        turn_rows(phase, turns, start, end)
        if c >= done:
            image[start:end, :] = transform_rows(dense, first, second, start, end)


def pinned(*arrays):
    return [pltpu.with_memory_space_constraint(x, pltpu.VMEM) for x in arrays]


def sent_rows(dense, first, second, start, end, image=None):
    grid_n = first.shape[0]
    vmem = pl.BlockSpec(memory_space=pltpu.VMEM)
    operands = [dense, first, second] + ([] if image is None else [image])
    return pl.pallas_call(
        functools.partial(sent_rows_kernel, start, end),
        out_shape=[
            pltpu.VMEM((grid_n, 2 * grid_n), jnp.float32),
            pltpu.VMEM((end - start, 2 * grid_n), jnp.bfloat16),
        ],
        in_specs=[vmem] * len(operands),
        out_specs=[vmem] * 2,
        input_output_aliases={} if image is None else {3: 0},
        compiler_params=pltpu.CompilerParams(vmem_limit_bytes=8 * 1024 * 1024),
        name="sent_rows",
    )(*pinned(*operands))


def other_rows(phase, dense, first, second, image, bounds, done):
    vmem = pl.BlockSpec(memory_space=pltpu.VMEM)
    return pl.pallas_call(
        functools.partial(other_rows_kernel, bounds, done),
        out_shape=[pltpu.VMEM(image.shape, jnp.float32), pltpu.VMEM(image.shape, jnp.float32)],
        in_specs=[vmem] * 5,
        out_specs=[vmem] * 2,
        input_output_aliases={4: 0},
        compiler_params=pltpu.CompilerParams(vmem_limit_bytes=8 * 1024 * 1024),
        name="other_rows",
    )(*pinned(phase, dense, first, second, image))


def dft_tables(grid_n):
    line = np.arange(grid_n)
    angle = (line[:, None] * line[None, :] % grid_n) * (2.0 * np.pi / grid_n)
    cos = np.cos(angle) / math.sqrt(grid_n)
    sin = np.sin(angle) / math.sqrt(grid_n)
    first = np.concatenate([cos, sin], axis=1)
    real = np.concatenate([cos, sin], axis=1).reshape(grid_n // SUB, SUB, 2 * grid_n)
    imag = np.concatenate([-sin, cos], axis=1).reshape(grid_n // SUB, SUB, 2 * grid_n)
    second = np.concatenate([real, imag], axis=1).reshape(2 * grid_n, 2 * grid_n)
    return first.astype(np.float32).astype(jnp.bfloat16), second.astype(np.float32).astype(jnp.bfloat16)


def send_up(part, hop):
    return lax.ppermute(part, "wa", [(hop - 1, hop)])


def turn_and_add(hop, start, incoming, image, turns, new_image, send=None):
    grid_n = image.shape[1] // 2
    rows = pl.ds(start, incoming.shape[0])
    re_cells, im_cells = pl.ds(0, grid_n), pl.ds(grid_n, grid_n)

    @pl.when(lax.axis_index("wa") == hop)
    def _():
        re = incoming[:, re_cells].astype(jnp.float32)
        im = incoming[:, im_cells].astype(jnp.float32)
        turn_re, turn_im = turns[rows, re_cells], turns[rows, im_cells]
        new_re = turn_re * re - turn_im * im + image[rows, re_cells]
        new_im = turn_re * im + turn_im * re + image[rows, im_cells]
        new_image[rows, re_cells] = new_re
        new_image[rows, im_cells] = new_im
        if send is not None:
            send[:, re_cells] = new_re.astype(jnp.bfloat16)
            send[:, im_cells] = new_im.astype(jnp.bfloat16)


def horner_kernel(hop, start, incoming, image, turns, send, new_image):
    turn_and_add(hop, start, incoming, image, turns, new_image, send)


def horner_step(hop, start, end, incoming, image, turns):
    vmem = pl.BlockSpec(memory_space=pltpu.VMEM)
    return pl.pallas_call(
        functools.partial(horner_kernel, hop, start),
        out_shape=[
            pltpu.VMEM((end - start, image.shape[1]), jnp.bfloat16),
            pltpu.VMEM(image.shape, jnp.float32),
        ],
        in_specs=[vmem] * 3,
        out_specs=[vmem] * 2,
        input_output_aliases={1: 1},
        compiler_params=pltpu.CompilerParams(vmem_limit_bytes=4 * 1024 * 1024),
        name="horner",
    )(*pinned(incoming, image, turns))


def last_kernel(hop, start, incoming, image, turns, *rest):
    new_image, result, sem = rest[-3:]
    turn_and_add(hop, start, incoming, image, turns, new_image)
    rows = pl.ds(start, incoming.shape[0])
    copy = pltpu.make_async_copy(new_image.at[rows, :], result.at[rows, :], sem)
    copy.start()
    copy.wait()


def last_step(hop, start, end, incoming, image, turns, result):
    vmem = pl.BlockSpec(memory_space=pltpu.VMEM)
    hbm = pl.BlockSpec(memory_space=pltpu.HBM)
    known = [] if result is None else [pltpu.with_memory_space_constraint(result, pltpu.HBM)]
    return pl.pallas_call(
        functools.partial(last_kernel, hop, start),
        out_shape=[pltpu.VMEM(image.shape, jnp.float32), pltpu.HBM(image.shape, jnp.float32)],
        in_specs=[vmem] * 3 + [hbm] * len(known),
        out_specs=[vmem, hbm],
        input_output_aliases={1: 0, **({3: 1} if known else {})},
        scratch_shapes=[pltpu.SemaphoreType.DMA],
        compiler_params=pltpu.CompilerParams(vmem_limit_bytes=4 * 1024 * 1024),
        name="last",
    )(*pinned(incoming, image, turns), *known)


def begin_kernel(start, image, send, _):
    @pl.when(lax.axis_index("wa") == 0)
    def _():
        send[...] = image[pl.ds(start, send.shape[0]), :].astype(jnp.bfloat16)


def begin_chain(start, end, image):
    vmem = pl.BlockSpec(memory_space=pltpu.VMEM)
    return pl.pallas_call(
        functools.partial(begin_kernel, start),
        out_shape=[
            pltpu.VMEM((end - start, image.shape[1]), jnp.bfloat16),
            pltpu.VMEM(image.shape, jnp.float32),
        ],
        in_specs=[vmem],
        out_specs=[vmem] * 2,
        input_output_aliases={0: 1},
        compiler_params=pltpu.CompilerParams(vmem_limit_bytes=4 * 1024 * 1024),
        name="begin",
    )(*pinned(image))


def on_device(visibilities, uv_angles, routes, offsets, pixel_phase):
    sub_count = visibilities.shape[0]
    count_vis = visibilities.shape[2]
    grid_n = pixel_phase.shape[1]
    planes = lax.axis_size("wa")
    owners = planes * lax.axis_size("facet")
    cap = max(2, (2 * sub_count + owners - 1) // owners)
    slots = owners * cap
    sent = pack(
        routes.T,
        offsets.T,
        uv_angles.transpose(1, 2, 0).reshape(2 * count_vis, sub_count),
        visibilities.transpose(1, 2, 0).reshape(2 * count_vis, sub_count),
        owners,
        cap,
    ).reshape(2 * slots, LANES)
    got = lax.all_to_all(sent, ("wa", "facet"), split_axis=0, concat_axis=0, tiled=True)
    digits = got.reshape(owners, 2, cap, LANES)[:, 1, :, : 2 * DIGITS + 1]
    digits = jnp.round(digits * (1.0 / DIGIT)).astype(jnp.int32)
    filled = jnp.sum(digits[:, :, 2 * DIGITS], axis=1)
    cells = digits[:, :, 0]
    for place in range(1, 2 * DIGITS):
        cells = cells + (digits[:, :, place] << (3 * place))
    cells = jnp.concatenate([cells.reshape(slots), filled])
    first, second = (jnp.asarray(x) for x in dft_tables(grid_n))
    dense, first, second = form_grid(cells, got, first, second, cap)

    units = grid_n // 16
    bounds = [0] + [16 * (units * sum(PARTS[: i + 1]) // sum(PARTS)) for i in range(len(PARTS))]
    count = len(PARTS)
    image, result, incoming = None, None, {}
    for c in range(EARLY):
        image, send = sent_rows(dense, first, second, bounds[c], bounds[c + 1], image)
        incoming[1, c] = send_up(send, 1)
    image, turns = other_rows(pixel_phase[0], dense, first, second, image, bounds, EARLY)

    def begin(c, image):
        if c < count:
            send, image = begin_chain(bounds[c], bounds[c + 1], image)
            incoming[1, c] = send_up(send, 1)
        return image

    for c in range(EARLY, AHEAD):
        image = begin(c, image)
    for beat in range(count + LAG * planes):
        for hop in range(1, planes):
            c = beat - LAG * (hop - 1)
            if 0 <= c < count:
                rows = bounds[c], bounds[c + 1]
                if hop + 1 < planes:
                    send, image = horner_step(hop, *rows, incoming[hop, c], image, turns)
                    incoming[hop + 1, c] = send_up(send, hop + 1)
                else:
                    image, result = last_step(hop, *rows, incoming[hop, c], image, turns, result)
                if hop == 1:
                    image = begin(c + AHEAD, image)
    return result.reshape(1, 1, grid_n, 2 * grid_n)


def solution(mesh):
    in_specs = (
        P(("wa", "facet"), None, None),
        P(("wa", "facet"), None, None),
        P(("wa", "facet"), None),
        P(("wa", "facet"), None),
        P("facet", None, None),
    )
    out_specs = P("wa", "facet", None, None)
    return jax.shard_map(
        on_device, mesh=mesh, in_specs=in_specs, out_specs=out_specs, check_vma=False
    )
```

```python
import functools
import math

import jax
import jax.numpy as jnp
import numpy as np
from jax import lax
from jax.experimental import pallas as pl
from jax.experimental.pallas import tpu as pltpu
from jax.sharding import PartitionSpec as P

SUB = 64
LANES = 128
ROWS = 8
GROUP = 8
PARTS = (7, 7, 7, 6, 5)
EARLY = 3
AHEAD = 3
LAG = 2
DIGITS = 3
DIGIT = 16.0
SINE = tuple(
    float(v)
    for v in np.linalg.lstsq(
        *(
            lambda x, w: (
                (x[:, None] ** np.arange(1, 10, 2)[None, :]) * w[:, None],
                np.sin(2 * np.pi * x) * w,
            )
        )(
            0.5 * np.cos(np.pi * (np.arange(2000) + 0.5) / 4000),
            np.ones(2000),
        ),
        rcond=None,
    )[0]
)


def sine_turns(turns):
    x = turns - jnp.round(turns)
    x2 = x * x
    total = jnp.full_like(x, SINE[-1])
    for c in SINE[-2::-1]:
        total = total * x2 + c
    return total * x


def pack_kernel(owners, cap, *refs):
    sources, out, places, sems = refs[:4], refs[4], refs[5:9], refs[9]
    copies = [
        pltpu.make_async_copy(source, place, sems.at[k])
        for k, (source, place) in enumerate(zip(sources, places))
    ]
    for copy in copies:
        copy.start()
    for copy in copies:
        copy.wait()
    routes, offsets, angles, vis = places
    rows = routes.shape[1]
    owner = lax.broadcasted_iota(jnp.int32, (owners, rows), 0)
    named = jnp.where(owner == routes[...], 1.0, 0.0)
    before = lax.broadcasted_iota(jnp.int32, (rows, rows), 0)
    until = before <= lax.broadcasted_iota(jnp.int32, (rows, rows), 1)
    until = jnp.where(until, 1.0, 0.0).astype(jnp.bfloat16)
    tally = jnp.dot(named.astype(jnp.bfloat16), until, preferred_element_type=jnp.float32)
    rank = jnp.sum(tally * named, axis=0, keepdims=True).astype(jnp.int32) - 1
    slot = routes[...] * cap + rank
    chosen = lax.broadcasted_iota(jnp.int32, (owners * cap, rows), 0) == slot
    chosen = jnp.where(chosen, 1.0, 0.0).astype(jnp.bfloat16)

    def pick(values):
        return lax.dot_general(
            chosen, values, (((1,), (1,)), ((), ())), preferred_element_type=jnp.float32
        )

    whole = angles[...]
    high = whole.astype(jnp.bfloat16)
    whole = whole - high.astype(jnp.float32)
    middle = whole.astype(jnp.bfloat16)
    low = (whole - middle.astype(jnp.float32)).astype(jnp.bfloat16)
    spot = lax.broadcasted_iota(jnp.int32, vis.shape, 0)
    digits = jnp.where(spot == 2 * DIGITS, 1, 0)
    for axis in range(2):
        for place in range(DIGITS):
            digit = (offsets[axis : axis + 1, :] >> (3 * place)) & 7
            digits = digits + jnp.where(spot == axis * DIGITS + place, digit, 0)
    digits = (digits.astype(jnp.float32) * DIGIT).astype(jnp.bfloat16)
    out[:, 0] = ((pick(high) + pick(middle)) + pick(low)).reshape(owners, cap, LANES)
    out[:, 1] = (pick(vis[...]) + pick(digits)).reshape(owners, cap, LANES)


def pack(routes, offsets, angles, vis, owners, cap):
    vmem = pl.BlockSpec(memory_space=pltpu.VMEM)
    return pl.pallas_call(
        functools.partial(pack_kernel, owners, cap),
        out_shape=pltpu.VMEM((owners, 2, cap, LANES), jnp.float32),
        compiler_params=pltpu.CompilerParams(vmem_limit_bytes=8 * 1024 * 1024),
        in_specs=[pl.BlockSpec(memory_space=pltpu.HBM)] * 4,
        out_specs=vmem,
        scratch_shapes=[
            *(pltpu.VMEM(x.shape, x.dtype) for x in (routes, offsets, angles, vis)),
            pltpu.SemaphoreType.DMA((4,)),
        ],
        name="pack",
    )(*(pltpu.with_memory_space_constraint(x, pltpu.HBM) for x in (routes, offsets, angles, vis)))


def grid_kernel(
    cap, cells, got, first_hbm, second_hbm, dense, first, second,
    turns_u, turns_v, amp_a, amp_b, grid, places, sems, *stages,
):
    slots = got.shape[0] // 2
    owners = slots // cap
    grid_n = dense.shape[0]
    blocks = grid_n // SUB
    group = stages[0].shape[0]
    bases, lefts, rights, pieces = (stages[2 * k : 2 * k + 2] for k in range(4))
    copies = [
        pltpu.make_async_copy(first_hbm, first, sems.at[0]),
        pltpu.make_async_copy(second_hbm, second, sems.at[1]),
    ]
    for copy in copies:
        copy.start()

    lane = lax.broadcasted_iota(jnp.int32, (ROWS, LANES), 1)
    low = lane < SUB
    row = lax.broadcasted_iota(jnp.int32, (ROWS, LANES), 0)
    quarter = jnp.where(low, 0.25, 0.0).astype(jnp.float32)
    sign = jnp.where(low, -1.0, 1.0).astype(jnp.float32)
    row_f = row.astype(jnp.float32)
    upper = row < ROWS // 2
    eights = ((row & (ROWS // 2 - 1)) * ROWS + ROWS).astype(jnp.float32)
    middle = SUB // ROWS // 2

    low_cap = lax.broadcasted_iota(jnp.int32, (cap, LANES), 1) < SUB

    def spread_out(i, count):
        angles = got[pl.ds(i * (2 * cap), cap), :]
        vis = got[pl.ds(i * (2 * cap) + cap, cap), :]
        vis = vis - jnp.round(vis * (1.0 / DIGIT)) * DIGIT
        rows = pl.ds(count, cap)
        both = angles * (1.0 / (2.0 * math.pi))
        swapped = pltpu.roll(both, SUB, 1)
        turns_u[rows, :] = jnp.where(low_cap, both, swapped)
        turns_v[rows, :] = jnp.where(low_cap, swapped, both)
        both = vis * (1.0 / math.sqrt(SUB))
        swapped = pltpu.roll(both, SUB, 1)
        amp_a[rows, :] = jnp.where(low_cap, both, swapped)
        amp_b[rows, :] = jnp.where(low_cap, swapped, both)
        for k in range(cap):
            places[count + k] = cells[i * cap + k]
        return count + cells[slots + i]

    count = lax.fori_loop(0, owners, spread_out, 0, unroll=8)
    for ref in (turns_u, turns_v, amp_a, amp_b):
        ref[pl.ds(count, 2 * group), :] = jnp.zeros((2 * group, LANES), jnp.float32)
    for k in range(2 * group):
        places[count + k] = 0
    pairs = jnp.maximum((count + 2 * group - 1) // (2 * group), 1)
    groups = 2 * pairs

    def offset_of(s, axis):
        return (places[s] >> (3 * DIGITS * axis)) & ((1 << (3 * DIGITS)) - 1)

    def clear(b, _):
        grid[pl.ds(b * grid_n, grid_n), :] = jnp.zeros((grid_n, LANES), grid.dtype)
        return 0

    lax.fori_loop(0, blocks + 1, clear, 0)

    def spread(ref, s):
        return jnp.broadcast_to(ref[pl.ds(s, 1), :], (ROWS, LANES))

    def find_bases(g, out):
        for i in range(group):
            s = g * group + i
            tu, tv = spread(turns_u, s), spread(turns_v, s)
            a, b = spread(amp_a, s), spread(amp_b, s)
            cs = sine_turns(tu * row_f + quarter)
            sc = pltpu.roll(cs, SUB, 1) * sign
            out[i, 0] = cs * a + sc * b
            out[i, 1] = sc * a - cs * b
            cs = sine_turns(tv * row_f + quarter)
            out[i, 2] = -(cs * sign)
            out[i, 3] = pltpu.roll(cs, SUB, 1)
            cs = sine_turns(jnp.where(upper, tu, tv) * eights + quarter)
            sc = pltpu.roll(cs, SUB, 1)
            out[i, 4] = jnp.where(low, cs, sc)
            out[i, 5] = jnp.where(low, sc, cs)

    def find_rows(source, left, right):
        for i in range(group):

            def line(k, j):
                return jnp.broadcast_to(source[i, k, j : j + 1, :], (ROWS, LANES))

            x, y = source[i, 0], source[i, 1]
            parts = [x]
            for j in range(middle):
                along, across = x * line(4, j), y * line(5, j)
                parts = [along - across] + parts
                if j + 1 < middle:
                    parts = parts + [along + across]
            left[i] = jnp.concatenate(parts, axis=0).astype(jnp.bfloat16)

            def keep(k, value_re, value_im):
                for place in (k, 2 * middle + k):
                    right[i, 0, place * ROWS : (place + 1) * ROWS, :] = value_re
                    right[i, 1, place * ROWS : (place + 1) * ROWS, :] = value_im

            x, y = source[i, 2], source[i, 3]
            keep(middle, x, y)
            for j in range(middle):
                wr, wi = line(4, middle + j), line(5, middle + j)
                xr, xi, yr, yi = x * wr, x * wi, y * wr, y * wi
                keep(middle - 1 - j, xr + yi, yr - xi)
                if j + 1 < middle:
                    keep(middle + 1 + j, xr - yi, yr + xi)

    def multiply(g, left, right, out):
        blank = jnp.zeros((SUB, LANES), jnp.bfloat16)
        for first_i in range(0, group, 2):
            halves = []
            for i in (first_i, first_i + 1):
                shift = offset_of(g * group + i, 1) & (SUB - 1)
                rows = pl.ds(SUB - shift, SUB)
                turned = jnp.concatenate([right[i, 0, rows, :], right[i, 1, rows, :]], axis=0)
                halves.append(turned.astype(jnp.bfloat16))
            upper_rows = jnp.concatenate([left[first_i], blank], axis=1)
            lower_rows = jnp.concatenate([blank, left[first_i + 1]], axis=1)
            both = lax.dot_general(
                jnp.concatenate([upper_rows, lower_rows], axis=0),
                jnp.concatenate(halves, axis=1),
                (((1,), (1,)), ((), ())),
                preferred_element_type=jnp.float32,
            )
            out[first_i] = both[:SUB]
            out[first_i + 1] = both[SUB:]

    cell = lax.broadcasted_iota(jnp.int32, (SUB, LANES), 1) & (SUB - 1)

    def add(g, formed):
        for i in range(group):
            s = g * group + i
            off_u, off_v = offset_of(s, 0), offset_of(s, 1)
            start = (off_v >> (SUB.bit_length() - 1)) * grid_n + off_u
            here = cell >= (off_v & (SUB - 1))
            places = [grid.at[pl.ds(start + side * grid_n, SUB), :] for side in range(2)]
            totals = [place[...] + formed[i] for place in places]
            pltpu.store(places[0], totals[0], mask=here)
            pltpu.store(places[1], totals[1], mask=~here)

    pieces[0][...] = jnp.zeros_like(pieces[0])
    lefts[1][...] = jnp.zeros_like(lefts[1])
    rights[1][...] = jnp.zeros_like(rights[1])
    find_bases(0, bases[0])

    def pair(p, _):
        for k in range(2):
            g = 2 * p + k
            add(jnp.maximum(g - 2, 0), pieces[k])
            multiply(jnp.maximum(g - 1, 0), lefts[1 - k], rights[1 - k], pieces[1 - k])
            find_rows(bases[k], lefts[k], rights[k])
            find_bases(jnp.minimum(g + 1, groups - 1), bases[1 - k])
        return 0

    lax.fori_loop(0, pairs, pair, 0)
    add(groups - 2, pieces[0])
    multiply(groups - 1, lefts[1], rights[1], pieces[1])
    add(groups - 1, pieces[1])

    for b in range(blocks):
        dense[:, b * LANES : (b + 1) * LANES] = grid[b * grid_n : (b + 1) * grid_n, :].astype(jnp.bfloat16)
    for copy in copies:
        copy.wait()


def form_grid(cells, got, first, second, cap):
    slots = got.shape[0] // 2
    grid_n = first.shape[0]
    blocks = grid_n // SUB
    group = math.gcd(slots // 2, GROUP)
    smem = pl.BlockSpec(memory_space=pltpu.SMEM)
    vmem = pl.BlockSpec(memory_space=pltpu.VMEM)
    hbm = pl.BlockSpec(memory_space=pltpu.HBM)
    line = pltpu.VMEM((slots + 2 * group, LANES), jnp.float32)
    stages = [
        pltpu.VMEM((group, 6, ROWS, LANES), jnp.float32),
        pltpu.VMEM((group, SUB, LANES), jnp.bfloat16),
        pltpu.VMEM((group, 2, 2 * SUB, LANES), jnp.float32),
        pltpu.VMEM((group, SUB, LANES), jnp.float32),
    ]
    return pl.pallas_call(
        functools.partial(grid_kernel, cap),
        out_shape=[
            pltpu.VMEM((grid_n, 2 * grid_n), jnp.bfloat16),
            pltpu.VMEM(first.shape, jnp.bfloat16),
            pltpu.VMEM(second.shape, jnp.bfloat16),
        ],
        in_specs=[smem, vmem, hbm, hbm],
        out_specs=[vmem] * 3,
        scratch_shapes=[
            line, line, line, line,
            pltpu.VMEM(((blocks + 1) * grid_n, LANES), jnp.float32),
            pltpu.SMEM((slots + 2 * group,), jnp.int32),
            pltpu.SemaphoreType.DMA((2,)),
            *(stage for stage in stages for _ in range(2)),
        ],
        compiler_params=pltpu.CompilerParams(vmem_limit_bytes=24 * 1024 * 1024),
        name="grid",
    )(
        cells,
        got,
        pltpu.with_memory_space_constraint(first, pltpu.HBM),
        pltpu.with_memory_space_constraint(second, pltpu.HBM),
    )


def transform_rows(dense, first, second, start, end):
    grid_n = dense.shape[0]
    rows = end - start
    both = jnp.concatenate([first[start:end, :grid_n], first[start:end, grid_n:]], axis=0)
    both = jnp.dot(both, dense[...], preferred_element_type=jnp.float32)
    sign = jnp.where(lax.broadcasted_iota(jnp.int32, (rows, LANES), 1) < SUB, -1.0, 1.0)
    half = [
        both[:rows, at : at + LANES] + pltpu.roll(both[rows:, at : at + LANES], SUB, 1) * sign
        for at in range(0, 2 * grid_n, LANES)
    ]
    half = jnp.concatenate(half, axis=1).astype(jnp.bfloat16)
    return jnp.dot(half, second[...], preferred_element_type=jnp.float32)


def sent_rows_kernel(start, end, dense, first, second, *rest):
    image, send = rest[-2:]
    rows = transform_rows(dense, first, second, start, end)
    image[start:end, :] = rows
    send[...] = rows.astype(jnp.bfloat16)


def turn_rows(phase, turns, start, end):
    grid_n = phase.shape[1]
    part = phase[start:end, :] * (1.0 / (2.0 * math.pi))
    turns[start:end, :grid_n] = sine_turns(part + 0.25)
    turns[start:end, grid_n:] = sine_turns(part)


def other_rows_kernel(bounds, done, phase, dense, first, second, _, image, turns):
    for c, (start, end) in enumerate(zip(bounds, bounds[1:])):
        turn_rows(phase, turns, start, end)
        if c >= done:
            image[start:end, :] = transform_rows(dense, first, second, start, end)


def pinned(*arrays):
    return [pltpu.with_memory_space_constraint(x, pltpu.VMEM) for x in arrays]


def sent_rows(dense, first, second, start, end, image=None):
    grid_n = first.shape[0]
    vmem = pl.BlockSpec(memory_space=pltpu.VMEM)
    operands = [dense, first, second] + ([] if image is None else [image])
    return pl.pallas_call(
        functools.partial(sent_rows_kernel, start, end),
        out_shape=[
            pltpu.VMEM((grid_n, 2 * grid_n), jnp.float32),
            pltpu.VMEM((end - start, 2 * grid_n), jnp.bfloat16),
        ],
        in_specs=[vmem] * len(operands),
        out_specs=[vmem] * 2,
        input_output_aliases={} if image is None else {3: 0},
        compiler_params=pltpu.CompilerParams(vmem_limit_bytes=8 * 1024 * 1024),
        name="sent_rows",
    )(*pinned(*operands))


def other_rows(phase, dense, first, second, image, bounds, done):
    vmem = pl.BlockSpec(memory_space=pltpu.VMEM)
    return pl.pallas_call(
        functools.partial(other_rows_kernel, bounds, done),
        out_shape=[pltpu.VMEM(image.shape, jnp.float32), pltpu.VMEM(image.shape, jnp.float32)],
        in_specs=[vmem] * 5,
        out_specs=[vmem] * 2,
        input_output_aliases={4: 0},
        compiler_params=pltpu.CompilerParams(vmem_limit_bytes=8 * 1024 * 1024),
        name="other_rows",
    )(*pinned(phase, dense, first, second, image))


def dft_tables(grid_n):
    line = np.arange(grid_n)
    angle = (line[:, None] * line[None, :] % grid_n) * (2.0 * np.pi / grid_n)
    cos = np.cos(angle) / math.sqrt(grid_n)
    sin = np.sin(angle) / math.sqrt(grid_n)
    first = np.concatenate([cos, sin], axis=1)
    real = np.concatenate([cos, sin], axis=1).reshape(grid_n // SUB, SUB, 2 * grid_n)
    imag = np.concatenate([-sin, cos], axis=1).reshape(grid_n // SUB, SUB, 2 * grid_n)
    second = np.concatenate([real, imag], axis=1).reshape(2 * grid_n, 2 * grid_n)
    return first.astype(np.float32).astype(jnp.bfloat16), second.astype(np.float32).astype(jnp.bfloat16)


def send_up(part, hop):
    return lax.ppermute(part, "wa", [(hop - 1, hop)])


def turn_and_add(hop, start, incoming, image, turns, new_image, send=None):
    grid_n = image.shape[1] // 2
    rows = pl.ds(start, incoming.shape[0])
    re_cells, im_cells = pl.ds(0, grid_n), pl.ds(grid_n, grid_n)

    @pl.when(lax.axis_index("wa") == hop)
    def _():
        re = incoming[:, re_cells].astype(jnp.float32)
        im = incoming[:, im_cells].astype(jnp.float32)
        turn_re, turn_im = turns[rows, re_cells], turns[rows, im_cells]
        new_re = turn_re * re - turn_im * im + image[rows, re_cells]
        new_im = turn_re * im + turn_im * re + image[rows, im_cells]
        new_image[rows, re_cells] = new_re
        new_image[rows, im_cells] = new_im
        if send is not None:
            send[:, re_cells] = new_re.astype(jnp.bfloat16)
            send[:, im_cells] = new_im.astype(jnp.bfloat16)


def horner_kernel(hop, start, incoming, image, turns, send, new_image):
    turn_and_add(hop, start, incoming, image, turns, new_image, send)


def horner_step(hop, start, end, incoming, image, turns):
    vmem = pl.BlockSpec(memory_space=pltpu.VMEM)
    return pl.pallas_call(
        functools.partial(horner_kernel, hop, start),
        out_shape=[
            pltpu.VMEM((end - start, image.shape[1]), jnp.bfloat16),
            pltpu.VMEM(image.shape, jnp.float32),
        ],
        in_specs=[vmem] * 3,
        out_specs=[vmem] * 2,
        input_output_aliases={1: 1},
        compiler_params=pltpu.CompilerParams(vmem_limit_bytes=4 * 1024 * 1024),
        name="horner",
    )(*pinned(incoming, image, turns))


def last_kernel(hop, start, incoming, image, turns, *rest):
    new_image, result, sem = rest[-3:]
    turn_and_add(hop, start, incoming, image, turns, new_image)
    rows = pl.ds(start, incoming.shape[0])
    copy = pltpu.make_async_copy(new_image.at[rows, :], result.at[rows, :], sem)
    copy.start()
    copy.wait()


def last_step(hop, start, end, incoming, image, turns, result):
    vmem = pl.BlockSpec(memory_space=pltpu.VMEM)
    hbm = pl.BlockSpec(memory_space=pltpu.HBM)
    known = [] if result is None else [pltpu.with_memory_space_constraint(result, pltpu.HBM)]
    return pl.pallas_call(
        functools.partial(last_kernel, hop, start),
        out_shape=[pltpu.VMEM(image.shape, jnp.float32), pltpu.HBM(image.shape, jnp.float32)],
        in_specs=[vmem] * 3 + [hbm] * len(known),
        out_specs=[vmem, hbm],
        input_output_aliases={1: 0, **({3: 1} if known else {})},
        scratch_shapes=[pltpu.SemaphoreType.DMA],
        compiler_params=pltpu.CompilerParams(vmem_limit_bytes=4 * 1024 * 1024),
        name="last",
    )(*pinned(incoming, image, turns), *known)


def begin_kernel(start, image, send, _):
    @pl.when(lax.axis_index("wa") == 0)
    def _():
        send[...] = image[pl.ds(start, send.shape[0]), :].astype(jnp.bfloat16)


def begin_chain(start, end, image):
    vmem = pl.BlockSpec(memory_space=pltpu.VMEM)
    return pl.pallas_call(
        functools.partial(begin_kernel, start),
        out_shape=[
            pltpu.VMEM((end - start, image.shape[1]), jnp.bfloat16),
            pltpu.VMEM(image.shape, jnp.float32),
        ],
        in_specs=[vmem],
        out_specs=[vmem] * 2,
        input_output_aliases={0: 1},
        compiler_params=pltpu.CompilerParams(vmem_limit_bytes=4 * 1024 * 1024),
        name="begin",
    )(*pinned(image))


def on_device(visibilities, uv_angles, routes, offsets, pixel_phase):
    sub_count = visibilities.shape[0]
    count_vis = visibilities.shape[2]
    grid_n = pixel_phase.shape[1]
    planes = lax.axis_size("wa")
    owners = planes * lax.axis_size("facet")
    cap = max(2, (2 * sub_count + owners - 1) // owners)
    slots = owners * cap
    sent = pack(
        routes.T,
        offsets.T,
        uv_angles.transpose(1, 2, 0).reshape(2 * count_vis, sub_count),
        visibilities.transpose(1, 2, 0).reshape(2 * count_vis, sub_count),
        owners,
        cap,
    ).reshape(2 * slots, LANES)
    got = lax.all_to_all(sent, ("wa", "facet"), split_axis=0, concat_axis=0, tiled=True)
    digits = got.reshape(owners, 2, cap, LANES)[:, 1, :, : 2 * DIGITS + 1]
    digits = jnp.round(digits * (1.0 / DIGIT)).astype(jnp.int32)
    filled = jnp.sum(digits[:, :, 2 * DIGITS], axis=1)
    cells = digits[:, :, 0]
    for place in range(1, 2 * DIGITS):
        cells = cells + (digits[:, :, place] << (3 * place))
    cells = jnp.concatenate([cells.reshape(slots), filled])
    first, second = (jnp.asarray(x) for x in dft_tables(grid_n))
    dense, first, second = form_grid(cells, got, first, second, cap)

    units = grid_n // 16
    bounds = [0] + [16 * (units * sum(PARTS[: i + 1]) // sum(PARTS)) for i in range(len(PARTS))]
    count = len(PARTS)
    image, result, incoming = None, None, {}
    for c in range(EARLY):
        image, send = sent_rows(dense, first, second, bounds[c], bounds[c + 1], image)
        incoming[1, c] = send_up(send, 1)
    image, turns = other_rows(pixel_phase[0], dense, first, second, image, bounds, EARLY)

    def begin(c, image):
        if c < count:
            send, image = begin_chain(bounds[c], bounds[c + 1], image)
            incoming[1, c] = send_up(send, 1)
        return image

    for c in range(EARLY, AHEAD):
        image = begin(c, image)
    for beat in range(count + LAG * planes):
        for hop in range(1, planes):
            c = beat - LAG * (hop - 1)
            if 0 <= c < count:
                rows = bounds[c], bounds[c + 1]
                if hop + 1 < planes:
                    send, image = horner_step(hop, *rows, incoming[hop, c], image, turns)
                    incoming[hop + 1, c] = send_up(send, hop + 1)
                else:
                    image, result = last_step(hop, *rows, incoming[hop, c], image, turns, result)
                if hop == 1:
                    image = begin(c + AHEAD, image)
    return result.reshape(1, 1, grid_n, 2 * grid_n)


def solution(mesh):
    in_specs = (
        P(("wa", "facet"), None, None),
        P(("wa", "facet"), None, None),
        P(("wa", "facet"), None),
        P(("wa", "facet"), None),
        P("facet", None, None),
    )
    out_specs = P("wa", "facet", None, None)
    return jax.shard_map(
        on_device, mesh=mesh, in_specs=in_specs, out_specs=out_specs, check_vma=False
    )
```
